512 devices in a mesh: sec: 128 (over z, y, core), tile: 4 (over x).
Axes of the slice: x: 4, y: 4, z: 16, core: 2. Of those that a mesh axis runs over, the one named last changes fastest.
Arguments:
- pixels: bfloat16 [128, 128, 4096], P('sec', 'tile'), may hold values from -6 to 6
- offsets: int32 [2, 2, 128, 128], P(None, None, 'sec', 'tile'), may hold values from -8 to 8
- connections: int32 [4, 128, 128], P(None, 'sec', 'tile'), may hold values from 0 to 127
- confidence: float32 [128, 128], P('sec', 'tile'), may hold values from 0.3 to 3
Outputs:
- measured: float32 [2, 2, 128, 128], P(None, None, 'sec', 'tile')
- displacement: float32 [2, 128, 128], P(None, 'sec', 'tile')
The draws below stay inside these ranges and needn't reach their ends.
All inputs are finite; a program needn't handle non-finite values.
Results may differ from the reference program's by a relative error of at most 0.00065.
Values may be sent and summed in bfloat16 or wider, within the bound.
No kernel may reach another device: no remote copies, remote signals or barrier semaphores. Data moves between devices by JAX's collectives and lax.ppermute only.
A program may use at most 64 MiB of HBM per device.

```python
import math
import jax
import jax.numpy as jnp
from jax import lax

PIX = 64
ITERS = 3
NODES = 128
SECTIONS = 128


def draw_confidence(key, part):
    key = jax.random.fold_in(key, 11)
    base = jax.random.uniform(key, (SECTIONS, NODES), jnp.float32, 0.3, 1.0)
    ramp = 1.0 + 2.0 * jnp.arange(SECTIONS, dtype=jnp.float32) / max(SECTIONS - 1, 1)
    return base * ramp[:, None]


def set_ends(values, rng, smallest, top_value):
    extent = values.shape
    index_at = [jax.random.randint(jax.random.fold_in(rng, axis), (), 0, extent[axis]) for axis in range(len(extent))]
    values = values.at[tuple(index_at)].set(smallest)
    longest = extent.index(max(extent))
    index_at[longest] = (index_at[longest] + 1) % extent[longest]
    return values.at[tuple(index_at)].set(top_value)


def steps_of(stream_key, dims, pieces, low, high):
    def one(axis_at, blocks):
        heights = jax.random.uniform(jax.random.fold_in(jax.random.fold_in(stream_key, 6), axis_at), (blocks,), jnp.float32, low / len(pieces), high / len(pieces))
        return jnp.repeat(jnp.exp(heights), dims[axis_at] // blocks).reshape((-1,) + (1,) * (len(dims) - axis_at - 1))

    gain = one(*pieces[0])
    for cut in pieces[1:]:
        gain = gain * one(*cut)
    return gain


def noise(rng, extent, spread, limit, cuts=(), kind=jnp.bfloat16):
    drawn = spread * jax.random.normal(rng, extent, jnp.float32)
    if cuts:
        drawn = drawn * steps_of(rng, extent, cuts, -0.22, 0.18)
    return jnp.clip(drawn, -limit, limit).astype(kind)


def setup_inputs(seed: int = 0) -> dict:
    streams_of = jax.random.split(jax.random.key(seed), 5)
    return {
        "pixels": noise(streams_of[0], (SECTIONS, NODES, PIX * PIX), 1.0, 6.0, ((0, 128), (1, 4))),
        "offsets": set_ends(jax.random.randint(streams_of[1], (2, 2, SECTIONS, NODES), -8, 9), jax.random.fold_in(streams_of[1], 1), -8, 8).astype(jnp.int32),
        "connections": set_ends(jax.random.randint(streams_of[2], (4, SECTIONS, NODES), 0, NODES), jax.random.fold_in(streams_of[2], 1), 0, NODES - 1).astype(jnp.int32),
        "confidence": draw_confidence(jax.random.fold_in(streams_of[4], 71), 0),
    }


stiff_plane = 1.0
anchor = 0.05
springs = ((1, 1.0), (2, 0.5))

def tables():
    positions = jnp.arange(PIX, dtype=jnp.int32)
    angles = jnp.mod(positions[:, None] * positions[None, :], PIX).astype(jnp.float32) * (2.0 * math.pi / PIX)
    cosine = jnp.cos(angles)
    sine = jnp.sin(angles)
    row_table = jnp.concatenate([cosine, sine], 1).astype(jnp.bfloat16)
    col_table = jnp.concatenate([cosine, sine], 0).astype(jnp.bfloat16)
    return (row_table, col_table)

def spectrum(patches, row_table, col_table):
    patch_count = patches.shape[0]
    rows = patches.reshape(patch_count * PIX, PIX)
    half_done = jnp.dot(rows, row_table, preferred_element_type=jnp.float32).astype(jnp.bfloat16)
    half_done = half_done.reshape(patch_count, PIX, 2 * PIX)
    full = jnp.einsum('km,bmc->bkc', col_table.astype(jnp.float32), half_done.astype(jnp.float32), precision=lax.Precision.HIGHEST)
    real_part = full[:, :PIX, :PIX] - full[:, PIX:, PIX:]
    imag_part = -(full[:, :PIX, PIX:] + full[:, PIX:, :PIX])
    return jnp.concatenate([real_part, imag_part], -1).astype(jnp.bfloat16)

def phases(shift_by):
    positions = jnp.arange(PIX, dtype=jnp.int32)
    nudges = jnp.array([-1, 0, 1], dtype=jnp.int32)
    target = shift_by[:, None] + nudges[None, :]
    angles = jnp.mod(target[:, :, None] * positions[None, None, :], PIX).astype(jnp.float32) * (2.0 * math.pi / PIX)
    return (jnp.cos(angles), jnp.sin(angles))

def patch_scores(spec_a, spec_b, offset_pair):
    full_a = spec_a.astype(jnp.float32)
    full_b = spec_b.astype(jnp.float32)
    energy_a = lax.optimization_barrier(jnp.sum(full_a * full_a, axis=(1, 2))) / PIX ** 4 + 1e-05
    energy_b = lax.optimization_barrier(jnp.sum(full_b * full_b, axis=(1, 2))) / PIX ** 4 + 1e-05
    real_a, imag_a = (full_a[..., :PIX], full_a[..., PIX:])
    real_b, imag_b = (full_b[..., :PIX], full_b[..., PIX:])
    cross = jnp.concatenate([real_a * real_b + imag_a * imag_b, imag_a * real_b - real_a * imag_b], -1)
    cos_col, sin_col = phases(offset_pair[1])
    upper = jnp.concatenate([cos_col, sin_col], 1)
    lower = jnp.concatenate([-sin_col, cos_col], 1)
    phase_table = jnp.concatenate([upper, lower], 2)
    partial_sum = jnp.einsum('bkc,bgc->bkg', cross, phase_table, precision=lax.Precision.HIGHEST)
    cos_row, sin_row = phases(offset_pair[0])
    corr = jnp.einsum('bfk,bke->bfe', cos_row, partial_sum[..., :3], precision=lax.Precision.HIGHEST)
    corr = corr - jnp.einsum('bfk,bke->bfe', sin_row, partial_sum[..., 3:], precision=lax.Precision.HIGHEST)
    corr = corr / PIX ** 2
    score = corr / (PIX * jnp.sqrt(energy_a * energy_b))[:, None, None]
    weights = score * score
    summed = 1.0 + lax.optimization_barrier(jnp.sum(weights, axis=(1, 2)))
    nudges = jnp.array([-1.0, 0.0, 1.0], dtype=jnp.float32)
    along_rows = lax.optimization_barrier(jnp.sum(weights * nudges[None, :, None], axis=(1, 2))) / summed
    along_cols = lax.optimization_barrier(jnp.sum(weights * nudges[None, None, :], axis=(1, 2))) / summed
    return jnp.stack([offset_pair[0].astype(jnp.float32) + along_rows, offset_pair[1].astype(jnp.float32) + along_cols])

def plane(field, connections):

    def section(values, node_links):
        neighbours = values[:, node_links]
        differ = values[:, None] - neighbours
        pulled = jnp.zeros((2, NODES), jnp.float32).at[:, node_links.reshape(-1)].add(-differ.reshape(2, -1))
        return differ.sum(1) + pulled
    return jax.vmap(section, in_axes=(1, 1), out_axes=1)(field, connections)

def chain_shift(field, distance):
    padding = jnp.zeros((field.shape[0], distance, NODES), jnp.float32)
    lower = jnp.concatenate([padding, field[:, :-distance]], 1)
    upper = jnp.concatenate([field[:, distance:], padding], 1)
    return (lower, upper)

def hessian(field, connections, confidence):
    order = jnp.arange(SECTIONS, dtype=jnp.int32)
    result = stiff_plane * plane(field, connections) + anchor * field
    for distance, spring in springs:
        in_chain = (order >= distance).astype(jnp.float32)[:, None]
        lower, upper = chain_shift(field, distance)
        term = in_chain * confidence * (field - lower)
        lower_t, upper_t = chain_shift(term, distance)
        result = result + spring * (term - upper_t)
    return result

def reference(pixels, offsets, connections, confidence):
    row_table, col_table = tables()
    empty = jnp.zeros((NODES, PIX, 2 * PIX), jnp.bfloat16)

    def one_section(carry, inputs):
        prior_one, prior_two = carry
        patches, offset_here = inputs
        spectra = spectrum(patches, row_table, col_table)
        near_one = patch_scores(spectra, prior_one, offset_here[0])
        near_two = patch_scores(spectra, prior_two, offset_here[1])
        return ((spectra, prior_one), jnp.stack([near_one, near_two]))
    carried, measured = lax.scan(one_section, (empty, empty), (pixels, jnp.transpose(offsets, (2, 0, 1, 3))))
    measured = jnp.transpose(measured, (1, 2, 0, 3))
    order = jnp.arange(SECTIONS, dtype=jnp.int32)
    rest = jnp.zeros((2, SECTIONS, NODES), jnp.float32)
    for distance, spring in springs:
        in_chain = (order >= distance).astype(jnp.float32)[:, None]
        term = in_chain * confidence * measured[distance - 1]
        lower_t, upper_t = chain_shift(term, distance)
        rest = rest + spring * (term - upper_t)
    displacement = jnp.zeros((2, SECTIONS, NODES), jnp.float32)
    gradient = -rest
    for step_index in range(ITERS):
        curved = hessian(gradient, connections, confidence)
        alpha = jnp.sum(gradient * gradient) / jnp.sum(gradient * curved)
        displacement = displacement - alpha * gradient
        gradient = gradient - alpha * curved
    return (measured, displacement)
```

```python
import jax
import jax.numpy as jnp
from jax import lax
from jax.experimental import pallas as pl
from jax.experimental.pallas import tpu as pltpu
from jax.sharding import Mesh
from jax.sharding import PartitionSpec as P

PIX = 64
LANES = 128
TILES = PIX * PIX // LANES
REACH = 4
ROWS = 16
PLANE = 8
WINDOW = 3 * PLANE
ANCHOR = 0.05
SPRINGS = ((1, 1.0), (2, 0.5))
SEC = ("z", "y", "core")
VMEM = pl.BlockSpec(memory_space=pltpu.VMEM)
SMEM = pl.BlockSpec(memory_space=pltpu.SMEM)


def lanes_of(rows):
    return lax.broadcasted_iota(jnp.int32, (rows, LANES), 1)


def sublanes_of(rows):
    return lax.broadcasted_iota(jnp.int32, (rows, LANES), 0)


def pick(values, index):
    return jnp.take_along_axis(values, index, axis=1, mode="promise_in_bounds")


def pick_rows(values, index):
    parts = [pick(values[8 * i : 8 * i + 8], index[8 * i : 8 * i + 8]) for i in range(values.shape[0] // 8)]
    return jnp.concatenate(parts, 0)


def shifted_tiles(tile_of, shift_rows, lane):
    steps = jnp.broadcast_to((shift_rows >> 1) + REACH, (ROWS, LANES))
    odd_high = jnp.logical_and(jnp.broadcast_to(shift_rows & 1, (ROWS, LANES)) == 1, lane >= PIX)
    tiles = [tile_of((j + REACH) % TILES) for j in range(TILES)]
    for bit in range(4):
        move = (steps & (1 << bit)) != 0
        tiles = [jnp.where(move, tiles[(j - (1 << bit)) % TILES], tiles[j]) for j in range(TILES)]
    return [jnp.where(odd_high, tiles[j - 1], tiles[j]) for j in range(TILES)]


def offsets_found(a_tile, b_tile, shift_rows, shift_cols):
    lane = lanes_of(ROWS)
    low = lane < PIX
    moved = shifted_tiles(b_tile, shift_rows, lane)
    half = (lane ^ (PIX * (shift_rows & 1))) & PIX
    index = [half | ((lane - shift_cols - e) & (PIX - 1)) for e in (-1, 0, 1)]
    rolled = lambda j: pltpu.roll(a_tile(j % TILES), PIX, 1)
    zero = jnp.zeros((ROWS, LANES), jnp.float32)
    sums = [[zero] * 3 for _ in range(3)]
    energy_a, energy_b = zero, zero
    before, here = rolled(TILES - 1), rolled(0)
    for j in range(TILES):
        after = rolled(j + 1)
        centre = a_tile(j)
        rows_a = (jnp.where(low, before, here), centre, jnp.where(low, here, after))
        cols_b = [pick_rows(moved[j], index[e]) for e in range(3)]
        for e1 in range(3):
            for e2 in range(3):
                sums[e1][e2] = sums[e1][e2] + rows_a[e1] * cols_b[e2]
        energy_a = energy_a + centre * centre
        energy_b = energy_b + cols_b[1] * cols_b[1]
        before, here = here, after
    total = lambda v: jnp.sum(v, axis=1, keepdims=True)
    scale = (total(energy_a) / PIX**2 + 1e-05) * (total(energy_b) / PIX**2 + 1e-05) * PIX**2
    weights = []
    for e1 in range(3):
        corr = [total(sums[e1][e2]) for e2 in range(3)]
        weights.append([c * c / scale for c in corr])
    row_sums = [weights[e][0] + weights[e][1] + weights[e][2] for e in range(3)]
    summed = 1.0 + row_sums[0] + row_sums[1] + row_sums[2]
    col_low = weights[0][0] + weights[1][0] + weights[2][0]
    col_high = weights[0][2] + weights[1][2] + weights[2][2]
    return (
        shift_rows.astype(jnp.float32) + (row_sums[2] - row_sums[0]) / summed,
        shift_cols.astype(jnp.float32) + (col_high - col_low) / summed,
    )


def match_kernel(place, own, partner, prev, shifts, extra, pay):
    first_core = place[0] == 0

    def group(g, row):
        rows = pl.ds(pl.multiple_of(ROWS * g, ROWS), ROWS)
        tile = lambda ref: lambda j: ref[rows, LANES * j : LANES * (j + 1)].astype(jnp.float32)

        def chosen(j):
            at = (rows, slice(LANES * j, LANES * (j + 1)))
            return jnp.where(first_core, own[at].astype(jnp.float32), prev[at].astype(jnp.float32))

        for pair, (a_tile, b_tile) in enumerate(((tile(own), tile(prev)), (tile(partner), chosen))):
            found = offsets_found(
                a_tile, b_tile, shifts[rows, 2 * pair : 2 * pair + 1], shifts[rows, 2 * pair + 1 : 2 * pair + 2]
            )
            for part in range(2):
                at = 32 * (2 * pair + part) + ROWS * g + sublanes_of(ROWS)
                row = row + jnp.where(lanes_of(ROWS) == at, found[part], 0.0)
        return row

    row = lax.fori_loop(0, 2, group, jnp.zeros((ROWS, LANES), jnp.float32))
    pay[...] = extra[...]
    pay[0:1, :] = jnp.sum(row, axis=0, keepdims=True)


def spread_kernel(own, below, above, out):
    lane = lanes_of(1)
    conf = jnp.where(
        lane < 32,
        own[2:3, :],
        jnp.where(
            lane < 64, pltpu.roll(below[2:3, :], 32, 1), jnp.where(lane < 96, pltpu.roll(above[2:3, :], 64, 1), 0.0)
        ),
    )
    rows = [own[0:2, :], below[0:2, :], above[0:2, :], conf, jnp.zeros((1, LANES), jnp.float32)]
    out[...] = jnp.broadcast_to(jnp.concatenate(rows, 0)[None], out.shape)


def relax_kernel(place, gathered, sums_out, fields_out, measured_out, links, left, pushed):
    lane = lanes_of(PLANE)
    sub = sublanes_of(PLANE)

    def assembled(row, quarter):
        total = jnp.zeros((PLANE, LANES), jnp.float32)
        for x in range(4):
            piece = gathered[pl.ds(8 * x + row, PLANE, stride=32), :]
            moved = pltpu.roll(piece, 32 * ((x - quarter) % 4), 1) if x != quarter else piece
            total = jnp.where(lane // 32 == x, moved, total)
        return total

    def window(rows_quarters):
        return jnp.concatenate([assembled(r, q) for r, q in rows_quarters], 0)

    def cores_swapped(values):
        even = sublanes_of(WINDOW) % 2 == 0
        return jnp.where(even, up(values, 1), down(values, 1))

    up = lambda v, k: pltpu.roll(v, v.shape[0] - k, 0)
    down = lambda v, k: pltpu.roll(v, k, 0)

    found = [window([(2, q), (0, q), (4, q)]) for q in range(4)]
    measured = {1: [cores_swapped(found[2]), cores_swapped(found[3])], 2: found[:2]}
    node_links = [window([(3, q), (1, q), (5, q)]).astype(jnp.int32) for q in range(4)]
    confidence = window([(6, 1), (6, 0), (6, 2)])
    section = PLANE * (place[0] - 1) + sublanes_of(WINDOW)
    chain = {d: jnp.where(section >= d, confidence, 0.0) for d, _ in SPRINGS}

    first, last = 4, 18
    node = lax.broadcasted_iota(jnp.int32, (LANES, LANES), 0)
    for s in range(first, last):
        ends = [jnp.where(node == node_links[j][s : s + 1], 1.0, 0.0) for j in range(4)]
        links[s - first] = ((ends[0] + ends[1]) + (ends[2] + ends[3])).astype(jnp.bfloat16)

    def pushed_along(field, begin, end):
        for c in range(2):
            rest = field[c]
            for part in range(3):
                rounded = rest.astype(jnp.bfloat16).astype(jnp.float32)
                left[pl.ds(2 * part + c, WINDOW, stride=8), :] = rounded
                rest = rest - rounded
        for s in range(begin, end):
            pushed[8 * s : 8 * s + 8, :] = lax.dot_general(
                left[8 * s : 8 * s + 8, :].astype(jnp.bfloat16),
                links[s - first],
                (((1,), (1,)), ((), ())),
                preferred_element_type=jnp.float32,
            )
        part = lambda k: pushed[pl.ds(k, WINDOW, stride=8), :]
        return [part(c) + part(2 + c) + part(4 + c) for c in range(2)]

    def image(field, begin, end, degree):
        back = pushed_along(field, begin, end)
        if degree is None:
            degree = pushed[pl.ds(6, WINDOW, stride=8), :]
        out = []
        for c in range(2):
            v = field[c]
            ahead = [pick_rows(v, node_links[j]) for j in range(4)]
            plane = (4.0 + degree) * v - ((ahead[0] + ahead[1]) + (ahead[2] + ahead[3])) - back[c]
            total = plane + ANCHOR * v
            for d, spring in SPRINGS:
                term = chain[d] * (v - down(v, d))
                total = total + spring * (term - up(term, d))
            out.append(total)
        return out, degree

    left[...] = jnp.ones_like(left)
    pushed[...] = jnp.zeros_like(pushed)
    start = []
    for c in range(2):
        total = jnp.zeros((WINDOW, LANES), jnp.float32)
        for d, spring in SPRINGS:
            term = chain[d] * measured[d][c]
            total = total + spring * (up(term, d) - term)
        start.append(total)
    once, degree = image(start, 4, 18, None)
    twice, _ = image(once, 6, 16, degree)

    mid = lambda v: v[PLANE : 2 * PLANE]
    dot = lambda a, b: mid(a[0]) * mid(b[0]) + mid(a[1]) * mid(b[1])
    sums = [dot(start, start), dot(start, once), dot(once, once), dot(once, twice), dot(twice, twice)]
    form = ANCHOR * sums[4]
    for c in range(2):
        v = twice[c]
        for j in range(4):
            differ = mid(v) - pick(mid(v), mid(node_links[j]))
            form = form + differ * differ
        for d, spring in SPRINGS:
            differ = mid(v - down(v, d))
            form = form + spring * mid(chain[d]) * differ * differ
    sums.append(form)
    rows = [jnp.sum(s, axis=0, keepdims=True) for s in sums]
    rows = jnp.concatenate(rows + [jnp.zeros((2, LANES), jnp.float32)], 0)
    totals = jnp.sum(rows, axis=1, keepdims=True)
    line = jnp.sum(jnp.where(lane == sub, totals, 0.0), axis=0, keepdims=True)
    sums_out[...] = jnp.broadcast_to(line[None], sums_out.shape)

    mine = sub == place[1]

    def own(v):
        row = jnp.sum(jnp.where(mine, mid(v), 0.0), axis=0, keepdims=True)
        return pltpu.roll(row, place[2], 1)

    fields = [own(f[c]) for f in (start, once, twice) for c in range(2)]
    fields_out[...] = jnp.concatenate(fields + [jnp.zeros((2, LANES), jnp.float32)], 0)
    for d in (1, 2):
        for c in range(2):
            measured_out[d - 1, c] = own(measured[d][c])[:, :32]


def finish_kernel(sums, fields, out):
    line = jnp.sum(sums[...], axis=0)
    lane = lanes_of(1)
    m = [jnp.sum(jnp.where(lane == k, line, 0.0), axis=1, keepdims=True) for k in range(6)]
    bounded = lambda top, below: jnp.clip(top / below, 0.0, 1.0 / ANCHOR)
    a0 = m[0] / m[1]
    norm = m[0] - 2.0 * a0 * m[1] + a0 * a0 * m[2]
    curve = m[1] - 2.0 * a0 * m[2] + a0 * a0 * m[3]
    a1 = bounded(norm, curve)
    p, q = a0 + a1, a0 * a1
    k1, k2, k3, k4 = -2.0 * p, p * p + 2.0 * q, -2.0 * p * q, q * q
    norm = m[0] + k1 * m[1] + k2 * m[2] + k3 * m[3] + k4 * m[4]
    curve = m[1] + k1 * m[2] + k2 * m[3] + k3 * m[4] + k4 * m[5]
    a2 = bounded(norm, curve)
    for c in range(2):
        v0, v1, v2 = (fields[2 * k + c : 2 * k + c + 1, :] for k in range(3))
        value = (q + a2 * p) * v1 - (p + a2) * v0 - (a2 * q) * v2
        out[c] = value[:, :32]


def on_device(pixels, offsets, connections, confidence):
    z, y, core, x = (lax.axis_index(name) for name in ("z", "y", "core", "x"))
    planes = lax.axis_size("z")
    count = planes * PLANE
    own = pixels[0]
    prev = lax.ppermute(own, SEC, [(i, i + 2) for i in range(count - 2)])
    swap = [(0, 1), (1, 0)]
    partner = lax.ppermute(own, "core", swap)
    partner_offsets = lax.ppermute(offsets[0, :, 0], "core", swap)
    shifts = jnp.concatenate([offsets[1, :, 0], partner_offsets], 0).T
    extra = jnp.zeros((8, LANES), jnp.float32)
    extra = extra.at[1].set(connections.reshape(LANES).astype(jnp.float32))
    extra = extra.at[2, :32].set(confidence[0])
    f32 = jnp.float32

    pay = pl.pallas_call(
        match_kernel,
        out_shape=jax.ShapeDtypeStruct((8, LANES), f32),
        in_specs=[SMEM] + [VMEM] * 5,
        out_specs=VMEM,
        name="match",
    )(core[None].astype(jnp.int32), own, partner, prev, shifts, extra)
    below = lax.ppermute(pay, "z", [(i, i + 1) for i in range(planes - 1)])
    above = lax.ppermute(pay, "z", [(i + 1, i) for i in range(planes - 1)])
    spread = pl.pallas_call(
        spread_kernel,
        out_shape=jax.ShapeDtypeStruct((32, 8, LANES), f32),
        in_specs=[VMEM] * 3,
        out_specs=VMEM,
        name="spread",
    )(pay, below, above)
    gathered = lax.all_to_all(spread, ("y", "core", "x"), 0, 0, tiled=True)
    place = jnp.stack([z, 2 * y + core, (LANES - 32 * x) % LANES]).astype(jnp.int32)
    sums, fields, measured = pl.pallas_call(
        relax_kernel,
        out_shape=(
            jax.ShapeDtypeStruct((planes, 1, LANES), f32),
            jax.ShapeDtypeStruct((8, LANES), f32),
            jax.ShapeDtypeStruct((2, 2, 1, 32), f32),
        ),
        in_specs=[SMEM, VMEM],
        out_specs=(VMEM, VMEM, VMEM),
        scratch_shapes=[
            pltpu.VMEM((14, LANES, LANES), jnp.bfloat16),
            pltpu.VMEM((WINDOW * 8, LANES), f32),
            pltpu.VMEM((WINDOW * 8, LANES), f32),
        ],
        name="relax",
    )(place, gathered.reshape(32 * 8, LANES))
    everywhere = lax.all_to_all(sums, "z", 0, 0, tiled=True)
    displacement = pl.pallas_call(
        finish_kernel,
        out_shape=jax.ShapeDtypeStruct((2, 1, 32), f32),
        in_specs=[VMEM] * 2,
        out_specs=VMEM,
        name="finish",
    )(everywhere, fields)
    return (measured, displacement)


def solution(mesh):
    tiles = mesh.shape["tile"]
    devices = mesh.devices.reshape(mesh.shape["sec"] // PLANE, PLANE // 2, 2, tiles)
    return jax.shard_map(
        on_device,
        mesh=Mesh(devices, ("z", "y", "core", "x")),
        in_specs=(P(SEC, "x", None), P(None, None, SEC, "x"), P(None, SEC, "x"), P(SEC, "x")),
        out_specs=(P(None, None, SEC, "x"), P(None, SEC, "x")),
        check_vma=False,
    )
```

```python
import jax
import jax.numpy as jnp
from jax import lax
from jax.experimental import pallas as pl
from jax.experimental.pallas import tpu as pltpu
from jax.sharding import Mesh
from jax.sharding import PartitionSpec as P

PIX = 64
LANES = 128
TILES = PIX * PIX // LANES
REACH = 4
ROWS = 16
PLANE = 8
WINDOW = 3 * PLANE
ANCHOR = 0.05
SPRINGS = ((1, 1.0), (2, 0.5))
SEC = ("z", "y", "core")
VMEM = pl.BlockSpec(memory_space=pltpu.VMEM)
SMEM = pl.BlockSpec(memory_space=pltpu.SMEM)


def kept(array):
    return pltpu.with_memory_space_constraint(array, pltpu.VMEM)


def lanes_of(rows):
    return lax.broadcasted_iota(jnp.int32, (rows, LANES), 1)


def sublanes_of(rows):
    return lax.broadcasted_iota(jnp.int32, (rows, LANES), 0)


def pick(values, index):
    return jnp.take_along_axis(values, index, axis=1, mode="promise_in_bounds")


def pick_rows(values, index):
    parts = [pick(values[8 * i : 8 * i + 8], index[8 * i : 8 * i + 8]) for i in range(values.shape[0] // 8)]
    return jnp.concatenate(parts, 0)


def shifted_tiles(tile_of, shift_rows, lane):
    steps = jnp.broadcast_to((shift_rows >> 1) + REACH, (ROWS, LANES))
    odd_high = jnp.logical_and(jnp.broadcast_to(shift_rows & 1, (ROWS, LANES)) == 1, lane >= PIX)
    tiles = [tile_of((j + REACH) % TILES) for j in range(TILES)]
    for bit in range(4):
        move = (steps & (1 << bit)) != 0
        tiles = [jnp.where(move, tiles[(j - (1 << bit)) % TILES], tiles[j]) for j in range(TILES)]
    return [jnp.where(odd_high, tiles[j - 1], tiles[j]) for j in range(TILES)]


def offsets_found(a_tile, b_tile, shift_rows, shift_cols):
    lane = lanes_of(ROWS)
    low = lane < PIX
    moved = shifted_tiles(b_tile, shift_rows, lane)
    half = (lane ^ (PIX * (shift_rows & 1))) & PIX
    index = [half | ((lane - shift_cols - e) & (PIX - 1)) for e in (-1, 0, 1)]
    rolled = lambda j: pltpu.roll(a_tile(j % TILES), PIX, 1)
    zero = jnp.zeros((ROWS, LANES), jnp.float32)
    sums = [[zero] * 3 for _ in range(3)]
    energy_a, energy_b = zero, zero
    before, here = rolled(TILES - 1), rolled(0)
    for j in range(TILES):
        after = rolled(j + 1)
        centre = a_tile(j)
        rows_a = (jnp.where(low, before, here), centre, jnp.where(low, here, after))
        cols_b = [pick_rows(moved[j], index[e]) for e in range(3)]
        for e1 in range(3):
            for e2 in range(3):
                sums[e1][e2] = sums[e1][e2] + rows_a[e1] * cols_b[e2]
        energy_a = energy_a + centre * centre
        energy_b = energy_b + cols_b[1] * cols_b[1]
        before, here = here, after
    total = lambda v: jnp.sum(v, axis=1, keepdims=True)
    scale = (total(energy_a) / PIX**2 + 1e-05) * (total(energy_b) / PIX**2 + 1e-05) * PIX**2
    weights = []
    for e1 in range(3):
        corr = [total(sums[e1][e2]) for e2 in range(3)]
        weights.append([c * c / scale for c in corr])
    row_sums = [weights[e][0] + weights[e][1] + weights[e][2] for e in range(3)]
    summed = 1.0 + row_sums[0] + row_sums[1] + row_sums[2]
    col_low = weights[0][0] + weights[1][0] + weights[2][0]
    col_high = weights[0][2] + weights[1][2] + weights[2][2]
    return (
        shift_rows.astype(jnp.float32) + (row_sums[2] - row_sums[0]) / summed,
        shift_cols.astype(jnp.float32) + (col_high - col_low) / summed,
    )


def match_kernel(place, own, partner, prev, shifts, extra, pay):
    first_core = place[0] == 0

    def group(g, row):
        rows = pl.ds(pl.multiple_of(ROWS * g, ROWS), ROWS)
        tile = lambda ref: lambda j: ref[rows, LANES * j : LANES * (j + 1)].astype(jnp.float32)

        def chosen(j):
            at = (rows, slice(LANES * j, LANES * (j + 1)))
            return jnp.where(first_core, own[at].astype(jnp.float32), prev[at].astype(jnp.float32))

        for pair, (a_tile, b_tile) in enumerate(((tile(own), tile(prev)), (tile(partner), chosen))):
            found = offsets_found(
                a_tile, b_tile, shifts[rows, 2 * pair : 2 * pair + 1], shifts[rows, 2 * pair + 1 : 2 * pair + 2]
            )
            for part in range(2):
                at = 32 * (2 * pair + part) + ROWS * g + sublanes_of(ROWS)
                row = row + jnp.where(lanes_of(ROWS) == at, found[part], 0.0)
        return row

    row = lax.fori_loop(0, 2, group, jnp.zeros((ROWS, LANES), jnp.float32))
    pay[...] = extra[...]
    pay[0:1, :] = jnp.sum(row, axis=0, keepdims=True)


def spread_kernel(own, below, above, out):
    lane = lanes_of(1)
    conf = jnp.where(
        lane < 32,
        own[2:3, :],
        jnp.where(
            lane < 64, pltpu.roll(below[2:3, :], 32, 1), jnp.where(lane < 96, pltpu.roll(above[2:3, :], 64, 1), 0.0)
        ),
    )
    rows = [own[0:2, :], below[0:2, :], above[0:2, :], conf, jnp.zeros((1, LANES), jnp.float32)]
    out[...] = jnp.broadcast_to(jnp.concatenate(rows, 0)[None], out.shape)


def relax_kernel(place, gathered, sums_out, fields_out, measured_out, links, left, pushed):
    lane = lanes_of(PLANE)
    sub = sublanes_of(PLANE)

    def assembled(row, quarter):
        total = jnp.zeros((PLANE, LANES), jnp.float32)
        for x in range(4):
            piece = gathered[pl.ds(8 * x + row, PLANE, stride=32), :]
            moved = pltpu.roll(piece, 32 * ((x - quarter) % 4), 1) if x != quarter else piece
            total = jnp.where(lane // 32 == x, moved, total)
        return total

    def window(rows_quarters):
        return jnp.concatenate([assembled(r, q) for r, q in rows_quarters], 0)

    def cores_swapped(values):
        even = sublanes_of(WINDOW) % 2 == 0
        return jnp.where(even, up(values, 1), down(values, 1))

    up = lambda v, k: pltpu.roll(v, v.shape[0] - k, 0)
    down = lambda v, k: pltpu.roll(v, k, 0)

    found = [window([(2, q), (0, q), (4, q)]) for q in range(4)]
    measured = {1: [cores_swapped(found[2]), cores_swapped(found[3])], 2: found[:2]}
    node_links = [window([(3, q), (1, q), (5, q)]).astype(jnp.int32) for q in range(4)]
    confidence = window([(6, 1), (6, 0), (6, 2)])
    section = PLANE * (place[0] - 1) + sublanes_of(WINDOW)
    chain = {d: jnp.where(section >= d, confidence, 0.0) for d, _ in SPRINGS}

    first, last = 4, 18
    node = lax.broadcasted_iota(jnp.int32, (LANES, LANES), 0)
    for s in range(first, last):
        ends = [jnp.where(node == node_links[j][s : s + 1], 1.0, 0.0) for j in range(4)]
        links[s - first] = ((ends[0] + ends[1]) + (ends[2] + ends[3])).astype(jnp.bfloat16)

    def pushed_along(field, begin, end):
        for c in range(2):
            rest = field[c]
            for part in range(3):
                rounded = rest.astype(jnp.bfloat16).astype(jnp.float32)
                left[pl.ds(2 * part + c, WINDOW, stride=8), :] = rounded
                rest = rest - rounded
        for s in range(begin, end):
            pushed[8 * s : 8 * s + 8, :] = lax.dot_general(
                left[8 * s : 8 * s + 8, :].astype(jnp.bfloat16),
                links[s - first],
                (((1,), (1,)), ((), ())),
                preferred_element_type=jnp.float32,
            )
        part = lambda k: pushed[pl.ds(k, WINDOW, stride=8), :]
        return [part(c) + part(2 + c) + part(4 + c) for c in range(2)]

    def image(field, begin, end, degree):
        back = pushed_along(field, begin, end)
        if degree is None:
            degree = pushed[pl.ds(6, WINDOW, stride=8), :]
        out = []
        for c in range(2):
            v = field[c]
            ahead = [pick_rows(v, node_links[j]) for j in range(4)]
            plane = (4.0 + degree) * v - ((ahead[0] + ahead[1]) + (ahead[2] + ahead[3])) - back[c]
            total = plane + ANCHOR * v
            for d, spring in SPRINGS:
                term = chain[d] * (v - down(v, d))
                total = total + spring * (term - up(term, d))
            out.append(total)
        return out, degree

    left[...] = jnp.ones_like(left)
    pushed[...] = jnp.zeros_like(pushed)
    start = []
    for c in range(2):
        total = jnp.zeros((WINDOW, LANES), jnp.float32)
        for d, spring in SPRINGS:
            term = chain[d] * measured[d][c]
            total = total + spring * (up(term, d) - term)
        start.append(total)
    once, degree = image(start, 4, 18, None)
    twice, _ = image(once, 6, 16, degree)

    mid = lambda v: v[PLANE : 2 * PLANE]
    dot = lambda a, b: mid(a[0]) * mid(b[0]) + mid(a[1]) * mid(b[1])
    sums = [dot(start, start), dot(start, once), dot(once, once), dot(once, twice), dot(twice, twice)]
    form = ANCHOR * sums[4]
    for c in range(2):
        v = twice[c]
        for j in range(4):
            differ = mid(v) - pick(mid(v), mid(node_links[j]))
            form = form + differ * differ
        for d, spring in SPRINGS:
            differ = mid(v - down(v, d))
            form = form + spring * mid(chain[d]) * differ * differ
    sums.append(form)
    rows = [jnp.sum(s, axis=0, keepdims=True) for s in sums]
    rows = jnp.concatenate(rows + [jnp.zeros((2, LANES), jnp.float32)], 0)
    totals = jnp.sum(rows, axis=1, keepdims=True)
    line = jnp.sum(jnp.where(lane == sub, totals, 0.0), axis=0, keepdims=True)
    sums_out[...] = jnp.broadcast_to(line[None], sums_out.shape)

    mine = sub == place[1]

    def own(v):
        row = jnp.sum(jnp.where(mine, mid(v), 0.0), axis=0, keepdims=True)
        return pltpu.roll(row, place[2], 1)

    fields = [own(f[c]) for f in (start, once, twice) for c in range(2)]
    fields_out[...] = jnp.concatenate(fields + [jnp.zeros((2, LANES), jnp.float32)], 0)
    for d in (1, 2):
        for c in range(2):
            measured_out[d - 1, c] = own(measured[d][c])[:, :32]


def finish_kernel(sums, fields, out):
    line = jnp.sum(sums[...], axis=0)
    lane = lanes_of(1)
    m = [jnp.sum(jnp.where(lane == k, line, 0.0), axis=1, keepdims=True) for k in range(6)]
    bounded = lambda top, below: jnp.clip(top / below, 0.0, 1.0 / ANCHOR)
    a0 = m[0] / m[1]
    norm = m[0] - 2.0 * a0 * m[1] + a0 * a0 * m[2]
    curve = m[1] - 2.0 * a0 * m[2] + a0 * a0 * m[3]
    a1 = bounded(norm, curve)
    p, q = a0 + a1, a0 * a1
    k1, k2, k3, k4 = -2.0 * p, p * p + 2.0 * q, -2.0 * p * q, q * q
    norm = m[0] + k1 * m[1] + k2 * m[2] + k3 * m[3] + k4 * m[4]
    curve = m[1] + k1 * m[2] + k2 * m[3] + k3 * m[4] + k4 * m[5]
    a2 = bounded(norm, curve)
    for c in range(2):
        v0, v1, v2 = (fields[2 * k + c : 2 * k + c + 1, :] for k in range(3))
        value = (q + a2 * p) * v1 - (p + a2) * v0 - (a2 * q) * v2
        out[c] = value[:, :32]


def on_device(pixels, offsets, connections, confidence):
    z, y, core, x = (lax.axis_index(name) for name in ("z", "y", "core", "x"))
    planes = lax.axis_size("z")
    count = planes * PLANE
    own = pixels[0]
    prev = lax.ppermute(own, SEC, [(i, i + 2) for i in range(count - 2)])
    swap = [(0, 1), (1, 0)]
    partner = lax.ppermute(own, "core", swap)
    partner_offsets = lax.ppermute(offsets[0, :, 0], "core", swap)
    shifts = jnp.concatenate([offsets[1, :, 0], partner_offsets], 0).T
    extra = jnp.zeros((8, LANES), jnp.float32)
    extra = extra.at[1].set(connections.reshape(LANES).astype(jnp.float32))
    extra = extra.at[2, :32].set(confidence[0])
    f32 = jnp.float32

    pay = pl.pallas_call(
        match_kernel,
        out_shape=pltpu.VMEM((8, LANES), f32),
        in_specs=[SMEM] + [VMEM] * 5,
        out_specs=VMEM,
        name="match",
    )(core[None].astype(jnp.int32), *[kept(v) for v in (own, partner, prev, shifts, extra)])
    below = lax.ppermute(pay, "z", [(i, i + 1) for i in range(planes - 1)])
    above = lax.ppermute(pay, "z", [(i + 1, i) for i in range(planes - 1)])
    spread = pl.pallas_call(
        spread_kernel,
        out_shape=pltpu.VMEM((32, 8, LANES), f32),
        in_specs=[VMEM] * 3,
        out_specs=VMEM,
        name="spread",
    )(kept(pay), kept(below), kept(above))
    gathered = lax.all_to_all(spread, ("y", "core", "x"), 0, 0, tiled=True)
    place = jnp.stack([z, 2 * y + core, (LANES - 32 * x) % LANES]).astype(jnp.int32)
    sums, fields, measured = pl.pallas_call(
        relax_kernel,
        out_shape=(
            pltpu.VMEM((planes, 1, LANES), f32),
            pltpu.VMEM((8, LANES), f32),
            jax.ShapeDtypeStruct((2, 2, 1, 32), f32),
        ),
        in_specs=[SMEM, VMEM],
        out_specs=(VMEM, VMEM, VMEM),
        scratch_shapes=[
            pltpu.VMEM((14, LANES, LANES), jnp.bfloat16),
            pltpu.VMEM((WINDOW * 8, LANES), f32),
            pltpu.VMEM((WINDOW * 8, LANES), f32),
        ],
        name="relax",
    )(place, kept(gathered.reshape(32 * 8, LANES)))
    turned = [[(i + planes // 2) % planes for i in range(planes)]]
    everywhere = lax.all_to_all(sums, "z", 0, 0, tiled=True, axis_index_groups=turned)
    displacement = pl.pallas_call(
        finish_kernel,
        out_shape=jax.ShapeDtypeStruct((2, 1, 32), f32),
        in_specs=[VMEM] * 2,
        out_specs=VMEM,
        name="finish",
    )(kept(everywhere), kept(fields))
    return (measured, displacement)


def solution(mesh):
    tiles = mesh.shape["tile"]
    devices = mesh.devices.reshape(mesh.shape["sec"] // PLANE, PLANE // 2, 2, tiles)
    return jax.shard_map(
        on_device,
        mesh=Mesh(devices, ("z", "y", "core", "x")),
        in_specs=(P(SEC, "x", None), P(None, None, SEC, "x"), P(None, SEC, "x"), P(SEC, "x")),
        out_specs=(P(None, None, SEC, "x"), P(None, SEC, "x")),
        check_vma=False,
    )
```

```python
import jax
import jax.numpy as jnp
from jax import lax
from jax.experimental import pallas as pl
from jax.experimental.pallas import tpu as pltpu
from jax.sharding import Mesh
from jax.sharding import PartitionSpec as P

PIX = 64
LANES = 128
TILES = PIX * PIX // LANES
REACH = 4
ROWS = 16
PLANE = 8
WINDOW = 3 * PLANE
ANCHOR = 0.05
SPRINGS = ((1, 1.0), (2, 0.5))
SEC = ("z", "y", "core")
VMEM = pl.BlockSpec(memory_space=pltpu.VMEM)
SMEM = pl.BlockSpec(memory_space=pltpu.SMEM)


def kept(array):
    return pltpu.with_memory_space_constraint(array, pltpu.VMEM)


def lanes_of(rows):
    return lax.broadcasted_iota(jnp.int32, (rows, LANES), 1)


def sublanes_of(rows):
    return lax.broadcasted_iota(jnp.int32, (rows, LANES), 0)


def pick(values, index):
    return jnp.take_along_axis(values, index, axis=1, mode="promise_in_bounds")


def pick_rows(values, index):
    parts = [pick(values[8 * i : 8 * i + 8], index[8 * i : 8 * i + 8]) for i in range(values.shape[0] // 8)]
    return jnp.concatenate(parts, 0)


def shifted_tiles(tile_of, shift_rows, lane):
    steps = jnp.broadcast_to((shift_rows >> 1) + REACH, (ROWS, LANES))
    odd_high = jnp.logical_and(jnp.broadcast_to(shift_rows & 1, (ROWS, LANES)) == 1, lane >= PIX)
    tiles = [tile_of((j + REACH) % TILES) for j in range(TILES)]
    for bit in range(4):
        move = (steps & (1 << bit)) != 0
        tiles = [jnp.where(move, tiles[(j - (1 << bit)) % TILES], tiles[j]) for j in range(TILES)]
    return [jnp.where(odd_high, tiles[j - 1], tiles[j]) for j in range(TILES)]


def offsets_found(a_tile, b_tile, shift_rows, shift_cols):
    lane = lanes_of(ROWS)
    low = lane < PIX
    moved = shifted_tiles(b_tile, shift_rows, lane)
    half = (lane ^ (PIX * (shift_rows & 1))) & PIX
    index = [half | ((lane - shift_cols - e) & (PIX - 1)) for e in (-1, 0, 1)]
    rolled = lambda j: pltpu.roll(a_tile(j % TILES), PIX, 1)
    zero = jnp.zeros((ROWS, LANES), jnp.float32)
    sums = [[zero] * 3 for _ in range(3)]
    energy_a, energy_b = zero, zero
    before, here = rolled(TILES - 1), rolled(0)
    for j in range(TILES):
        after = rolled(j + 1)
        centre = a_tile(j)
        rows_a = (jnp.where(low, before, here), centre, jnp.where(low, here, after))
        cols_b = [pick_rows(moved[j], index[e]) for e in range(3)]
        for e1 in range(3):
            for e2 in range(3):
                sums[e1][e2] = sums[e1][e2] + rows_a[e1] * cols_b[e2]
        energy_a = energy_a + centre * centre
        energy_b = energy_b + cols_b[1] * cols_b[1]
        before, here = here, after
    total = lambda v: jnp.sum(v, axis=1, keepdims=True)
    scale = (total(energy_a) / PIX**2 + 1e-05) * (total(energy_b) / PIX**2 + 1e-05) * PIX**2
    weights = []
    for e1 in range(3):
        corr = [total(sums[e1][e2]) for e2 in range(3)]
        weights.append([c * c / scale for c in corr])
    row_sums = [weights[e][0] + weights[e][1] + weights[e][2] for e in range(3)]
    summed = 1.0 + row_sums[0] + row_sums[1] + row_sums[2]
    col_low = weights[0][0] + weights[1][0] + weights[2][0]
    col_high = weights[0][2] + weights[1][2] + weights[2][2]
    return (
        shift_rows.astype(jnp.float32) + (row_sums[2] - row_sums[0]) / summed,
        shift_cols.astype(jnp.float32) + (col_high - col_low) / summed,
    )


def prep_kernel(pixels, offsets, connections, confidence, own, shifts, extra):
    own[...] = pixels[...]
    rows = sublanes_of(ROWS)
    lane = lanes_of(ROWS)
    for g in range(2):
        tile = jnp.zeros((ROWS, LANES), jnp.float32)
        for d in range(2):
            for part in range(2):
                row = offsets[d, part].astype(jnp.float32)
                chosen = jnp.where(lane[:, :32] == rows[:, :32] + ROWS * g, row, 0.0)
                tile = jnp.where(lane == 2 * d + part, jnp.sum(chosen, axis=1, keepdims=True), tile)
        shifts[ROWS * g : ROWS * (g + 1), :] = tile
    extra[...] = jnp.zeros_like(extra)
    for j in range(4):
        extra[1:2, 32 * j : 32 * (j + 1)] = connections[j].astype(jnp.float32)
    extra[2:3, 0:32] = confidence[...]


def match_kernel(place, own, partner, prev, own_offsets, partner_offsets, extra, pay):
    first_core = place[3] == 0

    def group(g, row):
        rows = pl.ds(pl.multiple_of(ROWS * g, ROWS), ROWS)
        tile = lambda ref: lambda j: ref[rows, LANES * j : LANES * (j + 1)].astype(jnp.float32)

        def chosen(j):
            at = (rows, slice(LANES * j, LANES * (j + 1)))
            return jnp.where(first_core, own[at].astype(jnp.float32), prev[at].astype(jnp.float32))

        own_shifts = own_offsets[rows, :].astype(jnp.int32)
        partner_shifts = partner_offsets[rows, :].astype(jnp.int32)
        work = ((tile(own), tile(prev), own_shifts[:, 2:4]), (tile(partner), chosen, partner_shifts[:, 0:2]))
        for pair, (a_tile, b_tile, shifts) in enumerate(work):
            found = offsets_found(a_tile, b_tile, shifts[:, 0:1], shifts[:, 1:2])
            for part in range(2):
                at = 32 * (2 * pair + part) + ROWS * g + sublanes_of(ROWS)
                row = row + jnp.where(lanes_of(ROWS) == at, found[part], 0.0)
        return row

    row = lax.fori_loop(0, 2, group, jnp.zeros((ROWS, LANES), jnp.float32))
    pay[...] = extra[...]
    pay[0:1, :] = jnp.sum(row, axis=0, keepdims=True)


def spread_kernel(place, own, odd_pairs, even_pairs, out):
    lane = lanes_of(1)
    even = place[0] % 2 == 0
    below = jnp.where(even, odd_pairs[...], even_pairs[...])
    above = jnp.where(even, even_pairs[...], odd_pairs[...])
    conf = jnp.where(
        lane < 32,
        own[2:3, :],
        jnp.where(
            lane < 64, pltpu.roll(below[2:3, :], 32, 1), jnp.where(lane < 96, pltpu.roll(above[2:3, :], 64, 1), 0.0)
        ),
    )
    rows = [own[0:2, :], below[0:2, :], above[0:2, :], conf, jnp.zeros((1, LANES), jnp.float32)]
    out[...] = jnp.broadcast_to(jnp.concatenate(rows, 0)[None], out.shape)


def relax_kernel(place, gathered, sums_out, fields_out, measured_out, links, left, pushed):
    lane = lanes_of(PLANE)
    sub = sublanes_of(PLANE)

    def assembled(row, quarter):
        total = jnp.zeros((PLANE, LANES), jnp.float32)
        for x in range(4):
            piece = gathered[pl.ds(8 * x + row, PLANE, stride=32), :]
            moved = pltpu.roll(piece, 32 * ((x - quarter) % 4), 1) if x != quarter else piece
            total = jnp.where(lane // 32 == x, moved, total)
        return total

    def window(rows_quarters):
        return jnp.concatenate([assembled(r, q) for r, q in rows_quarters], 0)

    def cores_swapped(values):
        even = sublanes_of(WINDOW) % 2 == 0
        return jnp.where(even, up(values, 1), down(values, 1))

    up = lambda v, k: pltpu.roll(v, v.shape[0] - k, 0)
    down = lambda v, k: pltpu.roll(v, k, 0)

    found = [window([(2, q), (0, q), (4, q)]) for q in range(4)]
    measured = {1: [cores_swapped(found[2]), cores_swapped(found[3])], 2: found[:2]}
    node_links = [window([(3, q), (1, q), (5, q)]).astype(jnp.int32) for q in range(4)]
    confidence = window([(6, 1), (6, 0), (6, 2)])
    section = PLANE * (place[0] - 1) + sublanes_of(WINDOW)
    chain = {d: jnp.where(section >= d, confidence, 0.0) for d, _ in SPRINGS}

    first, last = 4, 18
    node = lax.broadcasted_iota(jnp.int32, (LANES, LANES), 0)
    for s in range(first, last):
        ends = [jnp.where(node == node_links[j][s : s + 1], 1.0, 0.0) for j in range(4)]
        links[s - first] = ((ends[0] + ends[1]) + (ends[2] + ends[3])).astype(jnp.bfloat16)

    def pushed_along(field, begin, end):
        for c in range(2):
            rest = field[c]
            for part in range(3):
                rounded = rest.astype(jnp.bfloat16).astype(jnp.float32)
                left[pl.ds(2 * part + c, WINDOW, stride=8), :] = rounded
                rest = rest - rounded
        for s in range(begin, end):
            pushed[8 * s : 8 * s + 8, :] = lax.dot_general(
                left[8 * s : 8 * s + 8, :].astype(jnp.bfloat16),
                links[s - first],
                (((1,), (1,)), ((), ())),
                preferred_element_type=jnp.float32,
            )
        part = lambda k: pushed[pl.ds(k, WINDOW, stride=8), :]
        return [part(c) + part(2 + c) + part(4 + c) for c in range(2)]

    def image(field, begin, end, degree):
        back = pushed_along(field, begin, end)
        if degree is None:
            degree = pushed[pl.ds(6, WINDOW, stride=8), :]
        out = []
        for c in range(2):
            v = field[c]
            ahead = [pick_rows(v, node_links[j]) for j in range(4)]
            plane = (4.0 + degree) * v - ((ahead[0] + ahead[1]) + (ahead[2] + ahead[3])) - back[c]
            total = plane + ANCHOR * v
            for d, spring in SPRINGS:
                term = chain[d] * (v - down(v, d))
                total = total + spring * (term - up(term, d))
            out.append(total)
        return out, degree

    left[...] = jnp.ones_like(left)
    pushed[...] = jnp.zeros_like(pushed)
    start = []
    for c in range(2):
        total = jnp.zeros((WINDOW, LANES), jnp.float32)
        for d, spring in SPRINGS:
            term = chain[d] * measured[d][c]
            total = total + spring * (up(term, d) - term)
        start.append(total)
    once, degree = image(start, 4, 18, None)
    twice, _ = image(once, 6, 16, degree)

    mid = lambda v: v[PLANE : 2 * PLANE]
    dot = lambda a, b: mid(a[0]) * mid(b[0]) + mid(a[1]) * mid(b[1])
    sums = [dot(start, start), dot(start, once), dot(once, once), dot(once, twice), dot(twice, twice)]
    form = ANCHOR * sums[4]
    for c in range(2):
        v = twice[c]
        for j in range(4):
            differ = mid(v) - pick(mid(v), mid(node_links[j]))
            form = form + differ * differ
        for d, spring in SPRINGS:
            differ = mid(v - down(v, d))
            form = form + spring * mid(chain[d]) * differ * differ
    sums.append(form)
    rows = [jnp.sum(s, axis=0, keepdims=True) for s in sums]
    rows = jnp.concatenate(rows + [jnp.zeros((2, LANES), jnp.float32)], 0)
    totals = jnp.sum(rows, axis=1, keepdims=True)
    line = jnp.sum(jnp.where(lane == sub, totals, 0.0), axis=0, keepdims=True)
    sums_out[...] = jnp.broadcast_to(line[None], sums_out.shape)

    mine = sub == place[1]

    def own(v):
        row = jnp.sum(jnp.where(mine, mid(v), 0.0), axis=0, keepdims=True)
        return pltpu.roll(row, place[2], 1)

    fields = [own(f[c]) for f in (start, once, twice) for c in range(2)]
    fields_out[...] = jnp.concatenate(fields + [jnp.zeros((2, LANES), jnp.float32)], 0)
    for d in (1, 2):
        for c in range(2):
            measured_out[d - 1, c] = own(measured[d][c])[:, :32]


def finish_kernel(sums, fields, out):
    line = jnp.sum(sums[...], axis=0)
    lane = lanes_of(1)
    m = [jnp.sum(jnp.where(lane == k, line, 0.0), axis=1, keepdims=True) for k in range(6)]
    bounded = lambda top, below: jnp.clip(top / below, 0.0, 1.0 / ANCHOR)
    a0 = m[0] / m[1]
    norm = m[0] - 2.0 * a0 * m[1] + a0 * a0 * m[2]
    curve = m[1] - 2.0 * a0 * m[2] + a0 * a0 * m[3]
    a1 = bounded(norm, curve)
    p, q = a0 + a1, a0 * a1
    k1, k2, k3, k4 = -2.0 * p, p * p + 2.0 * q, -2.0 * p * q, q * q
    norm = m[0] + k1 * m[1] + k2 * m[2] + k3 * m[3] + k4 * m[4]
    curve = m[1] + k1 * m[2] + k2 * m[3] + k3 * m[4] + k4 * m[5]
    a2 = bounded(norm, curve)
    for c in range(2):
        v0, v1, v2 = (fields[2 * k + c : 2 * k + c + 1, :] for k in range(3))
        value = (q + a2 * p) * v1 - (p + a2) * v0 - (a2 * q) * v2
        out[c] = value[:, :32]


def on_device(pixels, offsets, connections, confidence):
    z, y, core, x = (lax.axis_index(name) for name in ("z", "y", "core", "x"))
    planes = lax.axis_size("z")
    count = planes * PLANE
    own = pixels[0]
    swap = [(0, 1), (1, 0)]
    prev = lax.ppermute(own, SEC, [(i, i + 2) for i in range(count - 2)])
    partner = lax.ppermute(own, "core", swap)
    f32 = jnp.float32
    place = jnp.stack([z, 2 * y + core, (LANES - 32 * x) % LANES, core]).astype(jnp.int32)
    held, shifts, extra = pl.pallas_call(
        prep_kernel,
        out_shape=(pltpu.VMEM((32, PIX * PIX), jnp.bfloat16), pltpu.VMEM((32, LANES), f32), pltpu.VMEM((8, LANES), f32)),
        in_specs=[VMEM] * 4,
        out_specs=(VMEM, VMEM, VMEM),
        name="prep",
    )(own, offsets, connections, confidence)
    partner_shifts = lax.ppermute(shifts, "core", swap)

    pay = pl.pallas_call(
        match_kernel,
        out_shape=pltpu.VMEM((8, LANES), f32),
        in_specs=[SMEM] + [VMEM] * 6,
        out_specs=VMEM,
        name="match",
    )(place, *[kept(v) for v in (held, partner, prev, shifts, partner_shifts, extra)])
    swaps = lambda first: [(i + d, i + 1 - d) for i in range(first, planes - 1, 2) for d in (0, 1)]
    odd_pairs = lax.ppermute(pay, "z", swaps(1))
    even_pairs = lax.ppermute(pay, "z", swaps(0))
    spread = pl.pallas_call(
        spread_kernel,
        out_shape=pltpu.VMEM((32, 8, LANES), f32),
        in_specs=[SMEM] + [VMEM] * 3,
        out_specs=VMEM,
        name="spread",
    )(place, kept(pay), kept(odd_pairs), kept(even_pairs))
    gathered = lax.all_to_all(spread, ("y", "core", "x"), 0, 0, tiled=True)
    sums, fields, measured = pl.pallas_call(
        relax_kernel,
        out_shape=(
            pltpu.VMEM((planes, 1, LANES), f32),
            pltpu.VMEM((8, LANES), f32),
            jax.ShapeDtypeStruct((2, 2, 1, 32), f32),
        ),
        in_specs=[SMEM, VMEM],
        out_specs=(VMEM, VMEM, VMEM),
        scratch_shapes=[
            pltpu.VMEM((14, LANES, LANES), jnp.bfloat16),
            pltpu.VMEM((WINDOW * 8, LANES), f32),
            pltpu.VMEM((WINDOW * 8, LANES), f32),
        ],
        name="relax",
    )(place, kept(gathered.reshape(32 * 8, LANES)))
    turned = [[(i + planes // 2) % planes for i in range(planes)]]
    everywhere = lax.all_to_all(sums, "z", 0, 0, tiled=True, axis_index_groups=turned)
    displacement = pl.pallas_call(
        finish_kernel,
        out_shape=jax.ShapeDtypeStruct((2, 1, 32), f32),
        in_specs=[VMEM] * 2,
        out_specs=VMEM,
        name="finish",
    )(kept(everywhere), kept(fields))
    return (measured, displacement)


def solution(mesh):
    tiles = mesh.shape["tile"]
    devices = mesh.devices.reshape(mesh.shape["sec"] // PLANE, PLANE // 2, 2, tiles)
    return jax.shard_map(
        on_device,
        mesh=Mesh(devices, ("z", "y", "core", "x")),
        in_specs=(P(SEC, "x", None), P(None, None, SEC, "x"), P(None, SEC, "x"), P(SEC, "x")),
        out_specs=(P(None, None, SEC, "x"), P(None, SEC, "x")),
        check_vma=False,
    )
```

```python
import jax
import jax.numpy as jnp
from jax import lax
from jax.experimental import pallas as pl
from jax.experimental.pallas import tpu as pltpu
from jax.sharding import Mesh
from jax.sharding import PartitionSpec as P

PIX = 64
LANES = 128
TILES = PIX * PIX // LANES
REACH = 4
ROWS = 16
HEAD = 24
SUMS = 11
PLANE = 8
WINDOW = 3 * PLANE
ANCHOR = 0.05
SPRINGS = ((1, 1.0), (2, 0.5))
SEC = ("z", "y", "core")
VMEM = pl.BlockSpec(memory_space=pltpu.VMEM)
SMEM = pl.BlockSpec(memory_space=pltpu.SMEM)


def kept(array):
    return pltpu.with_memory_space_constraint(array, pltpu.VMEM)


def lanes_of(rows):
    return lax.broadcasted_iota(jnp.int32, (rows, LANES), 1)


def sublanes_of(rows):
    return lax.broadcasted_iota(jnp.int32, (rows, LANES), 0)


def pick(values, index):
    return jnp.take_along_axis(values, index, axis=1, mode="promise_in_bounds")


def pick_rows(values, index):
    parts = [pick(values[8 * i : 8 * i + 8], index[8 * i : 8 * i + 8]) for i in range(values.shape[0] // 8)]
    return jnp.concatenate(parts, 0)


def shifted_tiles(tile_of, shift_rows, lane):
    steps = (shift_rows >> 1) + REACH
    odd_high = jnp.logical_and((shift_rows & 1) == 1, lane >= PIX)
    tiles = [tile_of((j + REACH) % TILES) for j in range(TILES)]
    for bit in range(4):
        move = (steps & (1 << bit)) != 0
        tiles = [jnp.where(move, tiles[(j - (1 << bit)) % TILES], tiles[j]) for j in range(TILES)]
    return [jnp.where(odd_high, tiles[j - 1], tiles[j]) for j in range(TILES)]


def products(a_tile, b_tile, shift_rows, shift_cols):
    lane = lanes_of(ROWS)
    low = lane < PIX
    moved = shifted_tiles(b_tile, shift_rows, lane)
    half = (lane ^ (PIX * (shift_rows & 1))) & PIX
    index = [half | ((lane - shift_cols - e) & (PIX - 1)) for e in (-1, 0, 1)]
    rolled = lambda j: pltpu.roll(a_tile(j % TILES), PIX, 1)
    sums = [jnp.zeros((ROWS, LANES), jnp.float32)] * SUMS
    before, here = rolled(TILES - 1), rolled(0)
    for j in range(TILES):
        after = rolled(j + 1)
        centre = a_tile(j)
        rows_a = (jnp.where(low, before, here), centre, jnp.where(low, here, after))
        cols_b = [pick_rows(moved[j], index[e]) for e in range(3)]
        terms = [rows_a[e1] * cols_b[e2] for e1 in range(3) for e2 in range(3)]
        terms += [centre * centre, cols_b[1] * cols_b[1]]
        sums = [total + term for total, term in zip(sums, terms)]
        before, here = here, after
    return sums


def tile_reader(refs, group):
    rows = slice(ROWS * group, ROWS * (group + 1))

    def tile(j):
        ref, j = (refs[0], j) if len(refs) == 1 or j < HEAD else (refs[1], j - HEAD)
        return ref[rows, LANES * j : LANES * (j + 1)].astype(jnp.float32)

    return tile


def pair_products(out, at, a_refs, b_refs, turn):
    for g in range(2):
        rows = slice(ROWS * g, ROWS * (g + 1))
        sums = products(tile_reader(a_refs, g), tile_reader(b_refs, g), turn(0, rows), turn(1, rows))
        for k in range(SUMS):
            out[k, at + ROWS * g : at + ROWS * (g + 1), :] = sums[k]


def own_turns(turn):
    return lambda part, rows: turn[32 * part + rows.start : 32 * part + rows.stop, :]


def sent_turns(tail):
    at = PIX * PIX - LANES * HEAD
    return lambda part, rows: (
        tail[rows, at + LANES * part : at + LANES * (part + 1)].astype(jnp.float32).astype(jnp.int32)
    )


def prep_kernel(pixels, offsets, connections, confidence, own, head, tail, turn, extra):
    cut = LANES * HEAD
    rest = PIX * PIX - cut
    own[...] = pixels[...]
    head[...] = pixels[:, 0:cut]
    tail[:, 0:rest] = pixels[:, cut:]
    patch = lax.broadcasted_iota(jnp.int32, (32, 32), 0)
    diagonal = patch == lax.broadcasted_iota(jnp.int32, (32, 32), 1)
    for d in range(2):
        for part in range(2):
            chosen = jnp.where(diagonal, offsets[d, part].astype(jnp.float32), 0.0)
            column = jnp.broadcast_to(jnp.sum(chosen, axis=1, keepdims=True), (32, LANES))
            if d == 0:
                tail[:, rest + LANES * part : rest + LANES * (part + 1)] = column.astype(jnp.bfloat16)
            else:
                turn[32 * part : 32 * (part + 1), :] = column.astype(jnp.int32)
    extra[...] = jnp.zeros_like(extra)
    for j in range(4):
        extra[1:2, 32 * j : 32 * (j + 1)] = connections[j].astype(jnp.float32)
    extra[2:3, 0:32] = confidence[...]


def chip_kernel(place, own, head, tail, ready):
    @pl.when(place[3] == 0)
    def _():
        pair_products(ready, 0, (head, tail), (own,), sent_turns(tail))


def match_kernel(place, head, tail, prev, own, turn, ready, extra, pay, sums):
    @pl.when(place[3] == 0)
    def _():
        sums[:, 32:64, :] = ready[...]

    @pl.when(place[3] != 0)
    def _():
        pair_products(sums, 32, (head, tail), (prev,), sent_turns(tail))

    pair_products(sums, 0, (own,), (prev,), own_turns(turn))
    total = [jnp.sum(sums[k], axis=1, keepdims=True) for k in range(SUMS)]
    scale = (total[9] / PIX**2 + 1e-05) * (total[10] / PIX**2 + 1e-05) * PIX**2
    inverse = 1.0 / scale
    weights = [[total[3 * e1 + e2] * total[3 * e1 + e2] * inverse for e2 in range(3)] for e1 in range(3)]
    row_sums = [weights[e][0] + weights[e][1] + weights[e][2] for e in range(3)]
    share = 1.0 / (1.0 + row_sums[0] + row_sums[1] + row_sums[2])
    col_low = weights[0][0] + weights[1][0] + weights[2][0]
    col_high = weights[0][2] + weights[1][2] + weights[2][2]
    shifts = [
        jnp.concatenate([turns(part, slice(0, 32)) for turns in (own_turns(turn), sent_turns(tail))], 0).astype(jnp.float32)
        for part in range(2)
    ]
    found_rows = shifts[0] + (row_sums[2] - row_sums[0]) * share
    found_cols = shifts[1] + (col_high - col_low) * share
    lane, pair = lanes_of(64), sublanes_of(64)
    line = jnp.where(lane == pair, found_rows, jnp.where(lane == 64 + pair, found_cols, 0.0))
    pay[...] = extra[...]
    pay[0:1, :] = jnp.sum(line, axis=0, keepdims=True)


def spread_kernel(place, own, odd_pairs, even_pairs, out):
    lane = lanes_of(1)
    even = place[0] % 2 == 0
    below = jnp.where(even, odd_pairs[...], even_pairs[...])
    above = jnp.where(even, even_pairs[...], odd_pairs[...])
    conf = jnp.where(
        lane < 32,
        own[2:3, :],
        jnp.where(
            lane < 64, pltpu.roll(below[2:3, :], 32, 1), jnp.where(lane < 96, pltpu.roll(above[2:3, :], 64, 1), 0.0)
        ),
    )
    rows = [own[0:2, :], below[0:2, :], above[0:2, :], conf, jnp.zeros((1, LANES), jnp.float32)]
    out[...] = jnp.broadcast_to(jnp.concatenate(rows, 0)[None], out.shape)


def relax_kernel(place, gathered, sums_out, fields_out, links, left, pushed):
    lane = lanes_of(PLANE)
    sub = sublanes_of(PLANE)

    def assembled(row, quarter):
        total = jnp.zeros((PLANE, LANES), jnp.float32)
        for x in range(4):
            piece = gathered[pl.ds(8 * x + row, PLANE, stride=32), :]
            moved = pltpu.roll(piece, 32 * ((x - quarter) % 4), 1) if x != quarter else piece
            total = jnp.where(lane // 32 == x, moved, total)
        return total

    def window(rows_quarters):
        return jnp.concatenate([assembled(r, q) for r, q in rows_quarters], 0)

    def cores_swapped(values):
        even = sublanes_of(WINDOW) % 2 == 0
        return jnp.where(even, up(values, 1), down(values, 1))

    up = lambda v, k: pltpu.roll(v, v.shape[0] - k, 0)
    down = lambda v, k: pltpu.roll(v, k, 0)

    found = [window([(2, q), (0, q), (4, q)]) for q in range(4)]
    measured = {1: [cores_swapped(found[1]), cores_swapped(found[3])], 2: [found[0], found[2]]}
    node_links = [window([(3, q), (1, q), (5, q)]).astype(jnp.int32) for q in range(4)]
    confidence = window([(6, 1), (6, 0), (6, 2)])
    section = PLANE * (place[0] - 1) + sublanes_of(WINDOW)
    chain = {d: jnp.where(section >= d, confidence, 0.0) for d, _ in SPRINGS}

    first, last = 4, 18
    node = lax.broadcasted_iota(jnp.int32, (LANES, LANES), 0)
    for s in range(first, last):
        ends = [jnp.where(node == node_links[j][s : s + 1], 1.0, 0.0) for j in range(4)]
        links[s - first] = ((ends[0] + ends[1]) + (ends[2] + ends[3])).astype(jnp.bfloat16)

    def pushed_along(field, begin, end):
        for c in range(2):
            rest = field[c]
            for part in range(3):
                rounded = rest.astype(jnp.bfloat16).astype(jnp.float32)
                left[pl.ds(2 * part + c, WINDOW, stride=8), :] = rounded
                rest = rest - rounded
        for s in range(begin, end):
            pushed[8 * s : 8 * s + 8, :] = lax.dot_general(
                left[8 * s : 8 * s + 8, :].astype(jnp.bfloat16),
                links[s - first],
                (((1,), (1,)), ((), ())),
                preferred_element_type=jnp.float32,
            )
        part = lambda k: pushed[pl.ds(k, WINDOW, stride=8), :]
        return [part(c) + part(2 + c) + part(4 + c) for c in range(2)]

    def image(field, begin, end, degree):
        back = pushed_along(field, begin, end)
        if degree is None:
            degree = pushed[pl.ds(6, WINDOW, stride=8), :]
        out = []
        for c in range(2):
            v = field[c]
            ahead = [pick_rows(v, node_links[j]) for j in range(4)]
            plane = (4.0 + degree) * v - ((ahead[0] + ahead[1]) + (ahead[2] + ahead[3])) - back[c]
            total = plane + ANCHOR * v
            for d, spring in SPRINGS:
                term = chain[d] * (v - down(v, d))
                total = total + spring * (term - up(term, d))
            out.append(total)
        return out, degree

    left[...] = jnp.ones_like(left)
    pushed[...] = jnp.zeros_like(pushed)
    start = []
    for c in range(2):
        total = jnp.zeros((WINDOW, LANES), jnp.float32)
        for d, spring in SPRINGS:
            term = chain[d] * measured[d][c]
            total = total + spring * (up(term, d) - term)
        start.append(total)
    once, degree = image(start, 4, 18, None)
    twice, _ = image(once, 6, 16, degree)

    mid = lambda v: v[PLANE : 2 * PLANE]
    dot = lambda a, b: mid(a[0]) * mid(b[0]) + mid(a[1]) * mid(b[1])
    sums = [dot(start, start), dot(start, once), dot(once, once), dot(once, twice), dot(twice, twice)]
    form = ANCHOR * sums[4]
    for c in range(2):
        v = twice[c]
        for j in range(4):
            differ = mid(v) - pick(mid(v), mid(node_links[j]))
            form = form + differ * differ
        for d, spring in SPRINGS:
            differ = mid(v - down(v, d))
            form = form + spring * mid(chain[d]) * differ * differ
    sums.append(form)
    rows = [jnp.sum(s, axis=0, keepdims=True) for s in sums]
    rows = jnp.concatenate(rows + [jnp.zeros((2, LANES), jnp.float32)], 0)
    totals = jnp.sum(rows, axis=1, keepdims=True)
    line = jnp.sum(jnp.where(lane == sub, totals, 0.0), axis=0, keepdims=True)
    sums_out[...] = jnp.broadcast_to(line[None], sums_out.shape)

    mine = sub == place[1]

    def own(v):
        row = jnp.sum(jnp.where(mine, mid(v), 0.0), axis=0, keepdims=True)
        return pltpu.roll(row, place[2], 1)

    fields = [own(f[c]) for f in (start, once, twice) for c in range(2)]
    fields += [own(measured[d][c]) for d in (1, 2) for c in range(2)]
    fields_out[...] = jnp.concatenate(fields + [jnp.zeros((6, LANES), jnp.float32)], 0)


def finish_kernel(sums, fields, measured_out, out):
    for d in range(2):
        for c in range(2):
            row = 6 + 2 * d + c
            measured_out[d, c] = fields[row : row + 1, 0:32]
    line = jnp.sum(sums[...], axis=0)
    lane = lanes_of(1)
    m = [jnp.sum(jnp.where(lane == k, line, 0.0), axis=1, keepdims=True) for k in range(6)]
    bounded = lambda top, below: jnp.clip(top / below, 0.0, 1.0 / ANCHOR)
    a0 = m[0] / m[1]
    norm = m[0] - 2.0 * a0 * m[1] + a0 * a0 * m[2]
    curve = m[1] - 2.0 * a0 * m[2] + a0 * a0 * m[3]
    a1 = bounded(norm, curve)
    p, q = a0 + a1, a0 * a1
    k1, k2, k3, k4 = -2.0 * p, p * p + 2.0 * q, -2.0 * p * q, q * q
    norm = m[0] + k1 * m[1] + k2 * m[2] + k3 * m[3] + k4 * m[4]
    curve = m[1] + k1 * m[2] + k2 * m[3] + k3 * m[4] + k4 * m[5]
    a2 = bounded(norm, curve)
    for c in range(2):
        v0, v1, v2 = (fields[2 * k + c : 2 * k + c + 1, :] for k in range(3))
        value = (q + a2 * p) * v1 - (p + a2) * v0 - (a2 * q) * v2
        out[c] = value[:, :32]


def on_device(pixels, offsets, connections, confidence):
    z, y, core, x = (lax.axis_index(name) for name in ("z", "y", "core", "x"))
    planes = lax.axis_size("z")
    count = planes * PLANE
    own = pixels[0]
    swap = [(0, 1), (1, 0)]
    prev = lax.ppermute(own, SEC, [(i, i + 2) for i in range(count - 2)])
    f32 = jnp.float32
    place = jnp.stack([z, 2 * y + core, (LANES - 32 * x) % LANES, core]).astype(jnp.int32)
    held, head, tail, turn, extra = pl.pallas_call(
        prep_kernel,
        out_shape=(
            pltpu.VMEM((32, PIX * PIX), jnp.bfloat16),
            pltpu.VMEM((32, LANES * HEAD), jnp.bfloat16),
            pltpu.VMEM((32, PIX * PIX - LANES * HEAD + 2 * LANES), jnp.bfloat16),
            pltpu.VMEM((64, LANES), jnp.int32),
            pltpu.VMEM((8, LANES), f32),
        ),
        in_specs=[VMEM] * 4,
        out_specs=(VMEM,) * 5,
        name="prep",
    )(own, offsets, connections, confidence)
    head, tail = (lax.ppermute(v, "core", swap) for v in (head, tail))
    ready = pl.pallas_call(
        chip_kernel,
        out_shape=pltpu.VMEM((SUMS, 32, LANES), f32),
        in_specs=[SMEM] + [VMEM] * 3,
        out_specs=VMEM,
        name="chip",
    )(place, kept(held), kept(head), kept(tail))
    pay = pl.pallas_call(
        match_kernel,
        out_shape=pltpu.VMEM((8, LANES), f32),
        in_specs=[SMEM] + [VMEM] * 7,
        out_specs=VMEM,
        scratch_shapes=[pltpu.VMEM((SUMS, 64, LANES), f32)],
        name="match",
    )(place, *[kept(v) for v in (head, tail, prev, held, turn, ready, extra)])
    swaps = lambda first: [(i + d, i + 1 - d) for i in range(first, planes - 1, 2) for d in (0, 1)]
    odd_pairs = lax.ppermute(pay, "z", swaps(1))
    even_pairs = lax.ppermute(pay, "z", swaps(0))
    spread = pl.pallas_call(
        spread_kernel,
        out_shape=pltpu.VMEM((32, 8, LANES), f32),
        in_specs=[SMEM] + [VMEM] * 3,
        out_specs=VMEM,
        name="spread",
    )(place, kept(pay), kept(odd_pairs), kept(even_pairs))
    gathered = lax.all_to_all(spread, ("y", "core", "x"), 0, 0, tiled=True)
    sums, fields = pl.pallas_call(
        relax_kernel,
        out_shape=(
            pltpu.VMEM((planes, 1, LANES), f32),
            pltpu.VMEM((16, LANES), f32),
        ),
        in_specs=[SMEM, VMEM],
        out_specs=(VMEM, VMEM),
        scratch_shapes=[
            pltpu.VMEM((14, LANES, LANES), jnp.bfloat16),
            pltpu.VMEM((WINDOW * 8, LANES), f32),
            pltpu.VMEM((WINDOW * 8, LANES), f32),
        ],
        name="relax",
    )(place, kept(gathered.reshape(32 * 8, LANES)))
    turned = [[(i + planes // 2) % planes for i in range(planes)]]
    everywhere = lax.all_to_all(sums, "z", 0, 0, tiled=True, axis_index_groups=turned)
    measured, displacement = pl.pallas_call(
        finish_kernel,
        out_shape=(jax.ShapeDtypeStruct((2, 2, 1, 32), f32), jax.ShapeDtypeStruct((2, 1, 32), f32)),
        in_specs=[VMEM] * 2,
        out_specs=(VMEM, VMEM),
        name="finish",
    )(kept(everywhere), kept(fields))
    return (measured, displacement)


def solution(mesh):
    tiles = mesh.shape["tile"]
    devices = mesh.devices.reshape(mesh.shape["sec"] // PLANE, PLANE // 2, 2, tiles)
    return jax.shard_map(
        on_device,
        mesh=Mesh(devices, ("z", "y", "core", "x")),
        in_specs=(P(SEC, "x", None), P(None, None, SEC, "x"), P(None, SEC, "x"), P(SEC, "x")),
        out_specs=(P(None, None, SEC, "x"), P(None, SEC, "x")),
        check_vma=False,
    )
```

```python
import jax
import jax.numpy as jnp
from jax import lax
from jax.experimental import pallas as pl
from jax.experimental.pallas import tpu as pltpu
from jax.sharding import Mesh
from jax.sharding import PartitionSpec as P

PIX = 64
LANES = 128
TILES = PIX * PIX // LANES
REACH = 4
ROWS = 16
HEAD = 24
SUMS = 11
PLANE = 8
LEADER = 22
WINDOW = 3 * PLANE
ANCHOR = 0.05
SPRINGS = ((1, 1.0), (2, 0.5))
SEC = ("z", "y", "core")
VMEM = pl.BlockSpec(memory_space=pltpu.VMEM)


def kept(array):
    return pltpu.with_memory_space_constraint(array, pltpu.VMEM)


def lanes_of(rows):
    return lax.broadcasted_iota(jnp.int32, (rows, LANES), 1)


def sublanes_of(rows):
    return lax.broadcasted_iota(jnp.int32, (rows, LANES), 0)


def pick(values, index):
    return jnp.take_along_axis(values, index, axis=1, mode="promise_in_bounds")


def pick_rows(values, index):
    parts = [pick(values[8 * i : 8 * i + 8], index[8 * i : 8 * i + 8]) for i in range(values.shape[0] // 8)]
    return jnp.concatenate(parts, 0)


def shifted_tiles(tile_of, shift_rows, lane):
    steps = (shift_rows >> 1) + REACH
    odd_high = jnp.logical_and((shift_rows & 1) == 1, lane >= PIX)
    tiles = [tile_of((j + REACH) % TILES) for j in range(TILES)]
    for bit in range(4):
        move = (steps & (1 << bit)) != 0
        tiles = [jnp.where(move, tiles[(j - (1 << bit)) % TILES], tiles[j]) for j in range(TILES)]
    return [jnp.where(odd_high, tiles[j - 1], tiles[j]) for j in range(TILES)]


def products(a_tile, b_tile, shift_rows, shift_cols):
    lane = lanes_of(ROWS)
    low = lane < PIX
    moved = shifted_tiles(b_tile, shift_rows, lane)
    half = (lane ^ (PIX * (shift_rows & 1))) & PIX
    index = [half | ((lane - shift_cols - e) & (PIX - 1)) for e in (-1, 0, 1)]
    rolled = lambda j: pltpu.roll(a_tile(j % TILES), PIX, 1)
    sums = [jnp.zeros((ROWS, LANES), jnp.float32)] * SUMS
    before, here = rolled(TILES - 1), rolled(0)
    for j in range(TILES):
        after = rolled(j + 1)
        centre = a_tile(j)
        rows_a = (jnp.where(low, before, here), centre, jnp.where(low, here, after))
        cols_b = [pick_rows(moved[j], index[e]) for e in range(3)]
        terms = [rows_a[e1] * cols_b[e2] for e1 in range(3) for e2 in range(3)]
        terms += [centre * centre, cols_b[1] * cols_b[1]]
        sums = [total + term for total, term in zip(sums, terms)]
        before, here = here, after
    return sums


def tile_reader(refs, group):
    rows = slice(ROWS * group, ROWS * (group + 1))

    def tile(j):
        ref, j = (refs[0], j) if len(refs) == 1 or j < HEAD else (refs[1], j - HEAD)
        return ref[rows, LANES * j : LANES * (j + 1)].astype(jnp.float32)

    return tile


def pair_products(out, at, a_refs, b_refs, turn):
    for g in range(2):
        rows = slice(ROWS * g, ROWS * (g + 1))
        sums = products(tile_reader(a_refs, g), tile_reader(b_refs, g), turn(0, rows), turn(1, rows))
        for k in range(SUMS):
            out[k, at + ROWS * g : at + ROWS * (g + 1), :] = sums[k]


def own_turns(turn):
    return lambda part, rows: turn[32 * part + rows.start : 32 * part + rows.stop, :]


def sent_turns(tail):
    at = PIX * PIX - LANES * HEAD
    return lambda part, rows: (
        tail[rows, at + LANES * part : at + LANES * (part + 1)].astype(jnp.float32).astype(jnp.int32)
    )


def prep_kernel(pixels, offsets, connections, confidence, own, head, tail, turn, extra):
    cut = LANES * HEAD
    rest = PIX * PIX - cut
    own[...] = pixels[...]
    head[...] = pixels[:, 0:cut]
    tail[:, 0:rest] = pixels[:, cut:]
    patch = lax.broadcasted_iota(jnp.int32, (32, 32), 0)
    diagonal = patch == lax.broadcasted_iota(jnp.int32, (32, 32), 1)
    for d in range(2):
        for part in range(2):
            chosen = jnp.where(diagonal, offsets[d, part].astype(jnp.float32), 0.0)
            column = jnp.broadcast_to(jnp.sum(chosen, axis=1, keepdims=True), (32, LANES))
            if d == 0:
                tail[:, rest + LANES * part : rest + LANES * (part + 1)] = column.astype(jnp.bfloat16)
            else:
                turn[32 * part : 32 * (part + 1), :] = column.astype(jnp.int32)
    extra[...] = jnp.zeros_like(extra)
    for j in range(4):
        extra[1:2, 32 * j : 32 * (j + 1)] = connections[j].astype(jnp.float32)
    for k in range(3):
        extra[2 + k : 3 + k, 32 * k : 32 * (k + 1)] = confidence[...]


def chip_kernel(own, head, tail, ready):
    @pl.when(lax.axis_index("core") == 0)
    def _():
        pair_products(ready, 0, (head, tail), (own,), sent_turns(tail))


def match_kernel(head, tail, prev, own, turn, ready, extra, pay, sums):
    core = lax.axis_index("core")

    @pl.when(core == 0)
    def _():
        sums[:, 32:64, :] = ready[...]

    @pl.when(core != 0)
    def _():
        pair_products(sums, 32, (head, tail), (prev,), sent_turns(tail))

    pair_products(sums, 0, (own,), (prev,), own_turns(turn))
    total = [jnp.sum(sums[k], axis=1, keepdims=True) for k in range(SUMS)]
    scale = (total[9] / PIX**2 + 1e-05) * (total[10] / PIX**2 + 1e-05) * PIX**2
    inverse = 1.0 / scale
    weights = [[total[3 * e1 + e2] * total[3 * e1 + e2] * inverse for e2 in range(3)] for e1 in range(3)]
    row_sums = [weights[e][0] + weights[e][1] + weights[e][2] for e in range(3)]
    share = 1.0 / (1.0 + row_sums[0] + row_sums[1] + row_sums[2])
    col_low = weights[0][0] + weights[1][0] + weights[2][0]
    col_high = weights[0][2] + weights[1][2] + weights[2][2]
    shifts = [
        jnp.concatenate([turns(part, slice(0, 32)) for turns in (own_turns(turn), sent_turns(tail))], 0).astype(jnp.float32)
        for part in range(2)
    ]
    found_rows = shifts[0] + (row_sums[2] - row_sums[0]) * share
    found_cols = shifts[1] + (col_high - col_low) * share
    lane, pair = lanes_of(64), sublanes_of(64)
    line = jnp.where(lane == pair, found_rows, jnp.where(lane == 64 + pair, found_cols, 0.0))
    pay[...] = extra[...]
    pay[0:1, :] = jnp.sum(line, axis=0, keepdims=True)


def relax_kernel(gathered, sums_out, fields_out, links, left, pushed):
    lane = lanes_of(PLANE)
    sub = sublanes_of(PLANE)

    z, y, core, x_own = (lax.axis_index(name) for name in ("z", "y", "core", "x"))
    even = z % 2 == 0

    def loaded(row):
        found = [gathered[pl.ds(8 * x + row, PLANE, stride=32), :] for x in range(4)]
        section, x = LEADER // 4, LEADER % 4
        first, other = found[0], found[x]
        found[0] = jnp.where(sub == 0, pltpu.roll(other, PLANE - section, 0), first)
        found[x] = jnp.where(sub == section, pltpu.roll(first, section, 0), other)
        return found

    def assembled(parts, quarter):
        total = jnp.zeros((PLANE, LANES), jnp.float32)
        for x in range(4):
            moved = pltpu.roll(parts[x], 32 * ((x - quarter) % 4), 1) if x != quarter else parts[x]
            total = jnp.where(lane // 32 == x, moved, total)
        return total

    def in_order(own, odd_pair, even_pair):
        return (jnp.where(even, odd_pair, even_pair), own, jnp.where(even, even_pair, odd_pair))

    def windows(row):
        parts = [in_order(*[loaded(row + 2 * k)[x] for k in range(3)]) for x in range(4)]
        join = lambda q: jnp.concatenate([assembled([parts[x][p] for x in range(4)], q) for p in range(3)], 0)
        return [join(q) for q in range(4)]

    def cores_swapped(values):
        even = sublanes_of(WINDOW) % 2 == 0
        return jnp.where(even, up(values, 1), down(values, 1))

    up = lambda v, k: pltpu.roll(v, v.shape[0] - k, 0)
    down = lambda v, k: pltpu.roll(v, k, 0)

    found = windows(0)
    measured = {1: [cores_swapped(found[1]), cores_swapped(found[3])], 2: [found[0], found[2]]}
    node_links = [links_of.astype(jnp.int32) for links_of in windows(1)]
    weights = loaded(6)
    confidence = jnp.concatenate(in_order(*[assembled(weights, q) for q in range(3)]), 0)
    section = PLANE * (z - 1) + sublanes_of(WINDOW)
    chain = {d: jnp.where(section >= d, confidence, 0.0) for d, _ in SPRINGS}

    first, last = 4, 18
    node = lax.broadcasted_iota(jnp.int32, (LANES, LANES), 0)
    for s in range(first, last):
        ends = [jnp.where(node == node_links[j][s : s + 1], 1.0, 0.0) for j in range(4)]
        links[s - first] = ((ends[0] + ends[1]) + (ends[2] + ends[3])).astype(jnp.bfloat16)

    def pushed_along(field, begin, end):
        for c in range(2):
            rest = field[c]
            for part in range(3):
                rounded = rest.astype(jnp.bfloat16).astype(jnp.float32)
                left[pl.ds(2 * part + c, WINDOW, stride=8), :] = rounded
                rest = rest - rounded
        for s in range(begin, end):
            pushed[8 * s : 8 * s + 8, :] = lax.dot_general(
                left[8 * s : 8 * s + 8, :].astype(jnp.bfloat16),
                links[s - first],
                (((1,), (1,)), ((), ())),
                preferred_element_type=jnp.float32,
            )
        part = lambda k: pushed[pl.ds(k, WINDOW, stride=8), :]
        return [part(c) + part(2 + c) + part(4 + c) for c in range(2)]

    def image(field, begin, end, degree):
        back = pushed_along(field, begin, end)
        if degree is None:
            degree = pushed[pl.ds(6, WINDOW, stride=8), :]
        out = []
        for c in range(2):
            v = field[c]
            ahead = [pick_rows(v, node_links[j]) for j in range(4)]
            plane = (4.0 + degree) * v - ((ahead[0] + ahead[1]) + (ahead[2] + ahead[3])) - back[c]
            total = plane + ANCHOR * v
            for d, spring in SPRINGS:
                term = chain[d] * (v - down(v, d))
                total = total + spring * (term - up(term, d))
            out.append(total)
        return out, degree

    left[...] = jnp.ones_like(left)
    pushed[...] = jnp.zeros_like(pushed)
    start = []
    for c in range(2):
        total = jnp.zeros((WINDOW, LANES), jnp.float32)
        for d, spring in SPRINGS:
            term = chain[d] * measured[d][c]
            total = total + spring * (up(term, d) - term)
        start.append(total)
    once, degree = image(start, 4, 18, None)
    twice, _ = image(once, 6, 16, degree)

    mid = lambda v: v[PLANE : 2 * PLANE]
    dot = lambda a, b: mid(a[0]) * mid(b[0]) + mid(a[1]) * mid(b[1])
    sums = [dot(start, start), dot(start, once), dot(once, once), dot(once, twice), dot(twice, twice)]
    form = ANCHOR * sums[4]
    for c in range(2):
        v = twice[c]
        for j in range(4):
            differ = mid(v) - pick(mid(v), mid(node_links[j]))
            form = form + differ * differ
        for d, spring in SPRINGS:
            differ = mid(v - down(v, d))
            form = form + spring * mid(chain[d]) * differ * differ
    sums.append(form)
    rows = [jnp.sum(s, axis=0, keepdims=True) for s in sums]
    rows = jnp.concatenate(rows + [jnp.zeros((2, LANES), jnp.float32)], 0)
    totals = jnp.sum(rows, axis=1, keepdims=True)
    line = jnp.sum(jnp.where(lane == sub, totals, 0.0), axis=0, keepdims=True)
    sums_out[...] = jnp.broadcast_to(line[None], sums_out.shape)

    mine = sub == 2 * y + core

    def own(v):
        row = jnp.sum(jnp.where(mine, mid(v), 0.0), axis=0, keepdims=True)
        return pltpu.roll(row, (LANES - 32 * x_own) % LANES, 1)

    fields = [own(f[c]) for f in (start, once, twice) for c in range(2)]
    fields += [own(measured[d][c]) for d in (1, 2) for c in range(2)]
    fields_out[...] = jnp.concatenate(fields + [jnp.zeros((6, LANES), jnp.float32)], 0)


def finish_kernel(sums, fields, measured_out, out):
    for d in range(2):
        for c in range(2):
            row = 6 + 2 * d + c
            measured_out[d, c] = fields[row : row + 1, 0:32]
    line = jnp.sum(sums[...], axis=0)
    lane = lanes_of(1)
    m = [jnp.sum(jnp.where(lane == k, line, 0.0), axis=1, keepdims=True) for k in range(6)]
    bounded = lambda top, below: jnp.clip(top / below, 0.0, 1.0 / ANCHOR)
    a0 = m[0] / m[1]
    norm = m[0] - 2.0 * a0 * m[1] + a0 * a0 * m[2]
    curve = m[1] - 2.0 * a0 * m[2] + a0 * a0 * m[3]
    a1 = bounded(norm, curve)
    p, q = a0 + a1, a0 * a1
    k1, k2, k3, k4 = -2.0 * p, p * p + 2.0 * q, -2.0 * p * q, q * q
    norm = m[0] + k1 * m[1] + k2 * m[2] + k3 * m[3] + k4 * m[4]
    curve = m[1] + k1 * m[2] + k2 * m[3] + k3 * m[4] + k4 * m[5]
    a2 = bounded(norm, curve)
    for c in range(2):
        v0, v1, v2 = (fields[2 * k + c : 2 * k + c + 1, :] for k in range(3))
        value = (q + a2 * p) * v1 - (p + a2) * v0 - (a2 * q) * v2
        out[c] = value[:, :32]


def on_device(pixels, offsets, connections, confidence):
    planes = lax.axis_size("z")
    count = planes * PLANE
    own = pixels[0]
    swap = [(0, 1), (1, 0)]
    prev = lax.ppermute(own, SEC, [(i, i + 2) for i in range(count - 2)])
    f32 = jnp.float32
    held, head, tail, turn, extra = pl.pallas_call(
        prep_kernel,
        out_shape=(
            pltpu.VMEM((32, PIX * PIX), jnp.bfloat16),
            pltpu.VMEM((32, LANES * HEAD), jnp.bfloat16),
            pltpu.VMEM((32, PIX * PIX - LANES * HEAD + 2 * LANES), jnp.bfloat16),
            pltpu.VMEM((64, LANES), jnp.int32),
            pltpu.VMEM((8, LANES), f32),
        ),
        in_specs=[VMEM] * 4,
        out_specs=(VMEM,) * 5,
        name="prep",
    )(own, offsets, connections, confidence)
    head, tail = (lax.ppermute(v, "core", swap) for v in (head, tail))
    ready = pl.pallas_call(
        chip_kernel,
        out_shape=pltpu.VMEM((SUMS, 32, LANES), f32),
        in_specs=[VMEM] * 3,
        out_specs=VMEM,
        name="chip",
    )(kept(held), kept(head), kept(tail))
    pay = pl.pallas_call(
        match_kernel,
        out_shape=pltpu.VMEM((8, LANES), f32),
        in_specs=[VMEM] * 7,
        out_specs=VMEM,
        scratch_shapes=[pltpu.VMEM((SUMS, 64, LANES), f32)],
        name="match",
    )(*[kept(v) for v in (head, tail, prev, held, turn, ready, extra)])
    swaps = lambda first: [(i + d, i + 1 - d) for i in range(first, planes - 1, 2) for d in (0, 1)]
    odd_pairs = lax.ppermute(pay, "z", swaps(1))
    even_pairs = lax.ppermute(pay, "z", swaps(0))
    weights = pay[2:3] + odd_pairs[3:4] + even_pairs[4:5]
    block = jnp.concatenate([pay[0:2], odd_pairs[0:2], even_pairs[0:2], weights, jnp.zeros((1, LANES), f32)], 0)
    order = list(range(4 * PLANE))
    order[0], order[LEADER] = LEADER, 0
    gathered = lax.all_to_all(
        jnp.broadcast_to(block, (4 * PLANE, 8, LANES)),
        ("y", "core", "x"),
        0,
        0,
        tiled=True,
        axis_index_groups=[order],
    )
    sums, fields = pl.pallas_call(
        relax_kernel,
        out_shape=(
            pltpu.VMEM((planes, 1, LANES), f32),
            pltpu.VMEM((16, LANES), f32),
        ),
        in_specs=[VMEM],
        out_specs=(VMEM, VMEM),
        scratch_shapes=[
            pltpu.VMEM((14, LANES, LANES), jnp.bfloat16),
            pltpu.VMEM((WINDOW * 8, LANES), f32),
            pltpu.VMEM((WINDOW * 8, LANES), f32),
        ],
        name="relax",
    )(kept(gathered.reshape(32 * 8, LANES)))
    turned = [[(i + planes // 2) % planes for i in range(planes)]]
    everywhere = lax.all_to_all(sums, "z", 0, 0, tiled=True, axis_index_groups=turned)
    measured, displacement = pl.pallas_call(
        finish_kernel,
        out_shape=(jax.ShapeDtypeStruct((2, 2, 1, 32), f32), jax.ShapeDtypeStruct((2, 1, 32), f32)),
        in_specs=[VMEM] * 2,
        out_specs=(VMEM, VMEM),
        name="finish",
    )(kept(everywhere), kept(fields))
    return (measured, displacement)


def solution(mesh):
    tiles = mesh.shape["tile"]
    devices = mesh.devices.reshape(mesh.shape["sec"] // PLANE, PLANE // 2, 2, tiles)
    return jax.shard_map(
        on_device,
        mesh=Mesh(devices, ("z", "y", "core", "x")),
        in_specs=(P(SEC, "x", None), P(None, None, SEC, "x"), P(None, SEC, "x"), P(SEC, "x")),
        out_specs=(P(None, None, SEC, "x"), P(None, SEC, "x")),
        check_vma=False,
    )
```

```python
import jax
import jax.numpy as jnp
from jax import lax
from jax.experimental import pallas as pl
from jax.experimental.pallas import tpu as pltpu
from jax.sharding import Mesh
from jax.sharding import PartitionSpec as P

PIX = 64
LANES = 128
TILES = PIX * PIX // LANES
REACH = 4
ROWS = 16
HEAD = 24
SUMS = 11
PLANE = 8
LEADER = 22
WINDOW = 3 * PLANE
ANCHOR = 0.05
SPRINGS = ((1, 1.0), (2, 0.5))
SEC = ("z", "y", "core")
VMEM = pl.BlockSpec(memory_space=pltpu.VMEM)


def kept(array):
    return pltpu.with_memory_space_constraint(array, pltpu.VMEM)


def lanes_of(rows):
    return lax.broadcasted_iota(jnp.int32, (rows, LANES), 1)


def sublanes_of(rows):
    return lax.broadcasted_iota(jnp.int32, (rows, LANES), 0)


def pick(values, index):
    return jnp.take_along_axis(values, index, axis=1, mode="promise_in_bounds")


def pick_rows(values, index):
    parts = [pick(values[8 * i : 8 * i + 8], index[8 * i : 8 * i + 8]) for i in range(values.shape[0] // 8)]
    return jnp.concatenate(parts, 0)


def shifted_tiles(tile_of, shift_rows, lane):
    steps = (shift_rows >> 1) + REACH
    odd_high = jnp.logical_and((shift_rows & 1) == 1, lane >= PIX)
    tiles = [tile_of((j + REACH) % TILES) for j in range(TILES)]
    for bit in range(4):
        move = (steps & (1 << bit)) != 0
        tiles = [jnp.where(move, tiles[(j - (1 << bit)) % TILES], tiles[j]) for j in range(TILES)]
    return [jnp.where(odd_high, tiles[j - 1], tiles[j]) for j in range(TILES)]


def products(a_tile, b_tile, shift_rows, shift_cols):
    lane = lanes_of(ROWS)
    low = lane < PIX
    moved = shifted_tiles(b_tile, shift_rows, lane)
    half = (lane ^ (PIX * (shift_rows & 1))) & PIX
    index = [half | ((lane - shift_cols - e) & (PIX - 1)) for e in (-1, 0, 1)]
    rolled = lambda j: pltpu.roll(a_tile(j % TILES), PIX, 1)
    sums = [jnp.zeros((ROWS, LANES), jnp.float32)] * SUMS
    before, here = rolled(TILES - 1), rolled(0)
    for j in range(TILES):
        after = rolled(j + 1)
        centre = a_tile(j)
        rows_a = (jnp.where(low, before, here), centre, jnp.where(low, here, after))
        cols_b = [pick_rows(moved[j], index[e]) for e in range(3)]
        terms = [rows_a[e1] * cols_b[e2] for e1 in range(3) for e2 in range(3)]
        terms += [centre * centre, cols_b[1] * cols_b[1]]
        sums = [total + term for total, term in zip(sums, terms)]
        before, here = here, after
    return sums


def tile_reader(refs, group):
    rows = slice(ROWS * group, ROWS * (group + 1))

    def tile(j):
        ref, j = (refs[0], j) if len(refs) == 1 or j < HEAD else (refs[1], j - HEAD)
        return ref[rows, LANES * j : LANES * (j + 1)].astype(jnp.float32)

    return tile


def pair_products(out, at, a_refs, b_refs, turn):
    for g in range(2):
        rows = slice(ROWS * g, ROWS * (g + 1))
        sums = products(tile_reader(a_refs, g), tile_reader(b_refs, g), turn(0, rows), turn(1, rows))
        for k in range(SUMS):
            out[k, at + ROWS * g : at + ROWS * (g + 1), :] = sums[k]


def own_turns(turn):
    return lambda part, rows: turn[32 * part + rows.start : 32 * part + rows.stop, :]


def sent_turns(tail):
    at = PIX * PIX - LANES * HEAD
    return lambda part, rows: (
        tail[rows, at + LANES * part : at + LANES * (part + 1)].astype(jnp.float32).astype(jnp.int32)
    )


def prep_kernel(pixels, offsets, connections, confidence, own, head, tail, turn, extra):
    cut = LANES * HEAD
    rest = PIX * PIX - cut
    own[...] = pixels[...]
    head[...] = pixels[:, 0:cut]
    tail[:, 0:rest] = pixels[:, cut:]
    patch = lax.broadcasted_iota(jnp.int32, (32, 32), 0)
    diagonal = patch == lax.broadcasted_iota(jnp.int32, (32, 32), 1)
    for d in range(2):
        for part in range(2):
            chosen = jnp.where(diagonal, offsets[d, part].astype(jnp.float32), 0.0)
            column = jnp.broadcast_to(jnp.sum(chosen, axis=1, keepdims=True), (32, LANES))
            if d == 0:
                tail[:, rest + LANES * part : rest + LANES * (part + 1)] = column.astype(jnp.bfloat16)
            else:
                turn[32 * part : 32 * (part + 1), :] = column.astype(jnp.int32)
    extra[...] = jnp.zeros_like(extra)
    for j in range(4):
        extra[1:2, 32 * j : 32 * (j + 1)] = connections[j].astype(jnp.float32)
    for k in range(3):
        extra[2 + k : 3 + k, 32 * k : 32 * (k + 1)] = confidence[...]


def chip_kernel(own, head, tail, ready):
    @pl.when(lax.axis_index("core") == 0)
    def _():
        pair_products(ready, 0, (head, tail), (own,), sent_turns(tail))


def match_kernel(head, tail, prev, own, turn, ready, extra, pay, sums):
    core = lax.axis_index("core")

    @pl.when(core == 0)
    def _():
        sums[:, 32:64, :] = ready[...]

    @pl.when(core != 0)
    def _():
        pair_products(sums, 32, (head, tail), (prev,), sent_turns(tail))

    pair_products(sums, 0, (own,), (prev,), own_turns(turn))
    total = [jnp.sum(sums[k], axis=1, keepdims=True) for k in range(SUMS)]
    scale = (total[9] / PIX**2 + 1e-05) * (total[10] / PIX**2 + 1e-05) * PIX**2
    inverse = 1.0 / scale
    weights = [[total[3 * e1 + e2] * total[3 * e1 + e2] * inverse for e2 in range(3)] for e1 in range(3)]
    row_sums = [weights[e][0] + weights[e][1] + weights[e][2] for e in range(3)]
    share = 1.0 / (1.0 + row_sums[0] + row_sums[1] + row_sums[2])
    col_low = weights[0][0] + weights[1][0] + weights[2][0]
    col_high = weights[0][2] + weights[1][2] + weights[2][2]
    shifts = [
        jnp.concatenate([turns(part, slice(0, 32)) for turns in (own_turns(turn), sent_turns(tail))], 0).astype(jnp.float32)
        for part in range(2)
    ]
    found_rows = shifts[0] + (row_sums[2] - row_sums[0]) * share
    found_cols = shifts[1] + (col_high - col_low) * share
    lane, pair = lanes_of(64), sublanes_of(64)
    line = jnp.where(lane == pair, found_rows, jnp.where(lane == 64 + pair, found_cols, 0.0))
    pay[...] = extra[...]
    pay[0:1, :] = jnp.sum(line, axis=0, keepdims=True)


def relax_kernel(gathered, sums_out, fields_out, links, left, pushed):
    lane = lanes_of(PLANE)
    sub = sublanes_of(PLANE)

    z, y, core, x_own = (lax.axis_index(name) for name in ("z", "y", "core", "x"))
    even = z % 2 == 0

    def loaded(row):
        found = [gathered[pl.ds(8 * x + row, PLANE, stride=32), :] for x in range(4)]
        section, x = LEADER // 4, LEADER % 4
        first, other = found[0], found[x]
        found[0] = jnp.where(sub == 0, pltpu.roll(other, PLANE - section, 0), first)
        found[x] = jnp.where(sub == section, pltpu.roll(first, section, 0), other)
        return found

    def assembled(parts, quarter):
        total = jnp.zeros((PLANE, LANES), jnp.float32)
        for x in range(4):
            moved = pltpu.roll(parts[x], 32 * ((x - quarter) % 4), 1) if x != quarter else parts[x]
            total = jnp.where(lane // 32 == x, moved, total)
        return total

    def in_order(own, odd_pair, even_pair):
        return (jnp.where(even, odd_pair, even_pair), own, jnp.where(even, even_pair, odd_pair))

    def windows(row):
        parts = [in_order(*[loaded(row + 2 * k)[x] for k in range(3)]) for x in range(4)]
        join = lambda q: jnp.concatenate([assembled([parts[x][p] for x in range(4)], q) for p in range(3)], 0)
        return [join(q) for q in range(4)]

    def cores_swapped(values):
        even = sublanes_of(WINDOW) % 2 == 0
        return jnp.where(even, up(values, 1), down(values, 1))

    up = lambda v, k: pltpu.roll(v, v.shape[0] - k, 0)
    down = lambda v, k: pltpu.roll(v, k, 0)

    found = windows(0)
    measured = {1: [cores_swapped(found[1]), cores_swapped(found[3])], 2: [found[0], found[2]]}
    node_links = [links_of.astype(jnp.int32) for links_of in windows(1)]
    weights = loaded(6)
    confidence = jnp.concatenate(in_order(*[assembled(weights, q) for q in range(3)]), 0)
    section = PLANE * (z - 1) + sublanes_of(WINDOW)
    chain = {d: jnp.where(section >= d, confidence, 0.0) for d, _ in SPRINGS}

    first, last = 4, 18
    node = lax.broadcasted_iota(jnp.int32, (LANES, LANES), 0)
    for s in range(first, last):
        ends = [jnp.where(node == node_links[j][s : s + 1], 1.0, 0.0) for j in range(4)]
        links[s - first] = ((ends[0] + ends[1]) + (ends[2] + ends[3])).astype(jnp.bfloat16)

    def pushed_along(field, begin, end):
        for c in range(2):
            rest = field[c]
            for part in range(3):
                rounded = rest.astype(jnp.bfloat16).astype(jnp.float32)
                left[pl.ds(2 * part + c, WINDOW, stride=8), :] = rounded
                rest = rest - rounded
        for s in range(begin, end):
            pushed[8 * s : 8 * s + 8, :] = lax.dot_general(
                left[8 * s : 8 * s + 8, :].astype(jnp.bfloat16),
                links[s - first],
                (((1,), (1,)), ((), ())),
                preferred_element_type=jnp.float32,
            )
        part = lambda k: pushed[pl.ds(k, WINDOW, stride=8), :]
        return [part(c) + part(2 + c) + part(4 + c) for c in range(2)]

    def image(field, begin, end, degree):
        back = pushed_along(field, begin, end)
        if degree is None:
            degree = pushed[pl.ds(6, WINDOW, stride=8), :]
        out = []
        for c in range(2):
            v = field[c]
            ahead = [pick_rows(v, node_links[j]) for j in range(4)]
            plane = (4.0 + degree) * v - ((ahead[0] + ahead[1]) + (ahead[2] + ahead[3])) - back[c]
            total = plane + ANCHOR * v
            for d, spring in SPRINGS:
                term = chain[d] * (v - down(v, d))
                total = total + spring * (term - up(term, d))
            out.append(total)
        return out, degree

    left[...] = jnp.ones_like(left)
    pushed[...] = jnp.zeros_like(pushed)
    start = []
    for c in range(2):
        total = jnp.zeros((WINDOW, LANES), jnp.float32)
        for d, spring in SPRINGS:
            term = chain[d] * measured[d][c]
            total = total + spring * (up(term, d) - term)
        start.append(total)
    once, degree = image(start, 4, 18, None)
    twice, _ = image(once, 6, 16, degree)

    mid = lambda v: v[PLANE : 2 * PLANE]
    dot = lambda a, b: mid(a[0]) * mid(b[0]) + mid(a[1]) * mid(b[1])
    sums = [dot(start, start), dot(start, once), dot(once, once), dot(once, twice), dot(twice, twice)]
    form = ANCHOR * sums[4]
    for c in range(2):
        v = twice[c]
        for j in range(4):
            differ = mid(v) - pick(mid(v), mid(node_links[j]))
            form = form + differ * differ
        for d, spring in SPRINGS:
            differ = mid(v - down(v, d))
            form = form + spring * mid(chain[d]) * differ * differ
    sums.append(form)
    rows = [jnp.sum(s, axis=0, keepdims=True) for s in sums]
    rows = jnp.concatenate(rows + [jnp.zeros((2, LANES), jnp.float32)], 0)
    totals = jnp.sum(rows, axis=1, keepdims=True)
    line = jnp.sum(jnp.where(lane == sub, totals, 0.0), axis=0, keepdims=True)
    sums_out[...] = jnp.broadcast_to(line[None], sums_out.shape)

    mine = sub == 2 * y + core

    def own(v):
        row = jnp.sum(jnp.where(mine, mid(v), 0.0), axis=0, keepdims=True)
        return pltpu.roll(row, (LANES - 32 * x_own) % LANES, 1)

    fields = [own(f[c]) for f in (start, once, twice) for c in range(2)]
    fields += [own(measured[d][c]) for d in (1, 2) for c in range(2)]
    fields_out[...] = jnp.concatenate(fields + [jnp.zeros((6, LANES), jnp.float32)], 0)


def finish_kernel(sums, fields, measured_out, out):
    for d in range(2):
        for c in range(2):
            row = 6 + 2 * d + c
            measured_out[d, c] = fields[row : row + 1, 0:32]
    line = jnp.sum(sums[...], axis=0)
    lane = lanes_of(1)
    m = [jnp.sum(jnp.where(lane == k, line, 0.0), axis=1, keepdims=True) for k in range(6)]
    bounded = lambda top, below: jnp.clip(top / below, 0.0, 1.0 / ANCHOR)
    a0 = m[0] / m[1]
    norm = m[0] - 2.0 * a0 * m[1] + a0 * a0 * m[2]
    curve = m[1] - 2.0 * a0 * m[2] + a0 * a0 * m[3]
    a1 = bounded(norm, curve)
    p, q = a0 + a1, a0 * a1
    k1, k2, k3, k4 = -2.0 * p, p * p + 2.0 * q, -2.0 * p * q, q * q
    norm = m[0] + k1 * m[1] + k2 * m[2] + k3 * m[3] + k4 * m[4]
    curve = m[1] + k1 * m[2] + k2 * m[3] + k3 * m[4] + k4 * m[5]
    a2 = bounded(norm, curve)
    for c in range(2):
        v0, v1, v2 = (fields[2 * k + c : 2 * k + c + 1, :] for k in range(3))
        value = (q + a2 * p) * v1 - (p + a2) * v0 - (a2 * q) * v2
        out[c] = value[:, :32]


def on_device(pixels, offsets, connections, confidence):
    planes = lax.axis_size("z")
    count = planes * PLANE
    own = pixels[0]
    swap = [(0, 1), (1, 0)]
    prev = lax.ppermute(own, SEC, [(i, i + 2) for i in range(count - 2)])
    f32 = jnp.float32
    held, head, tail, turn, extra = pl.pallas_call(
        prep_kernel,
        out_shape=(
            pltpu.VMEM((32, PIX * PIX), jnp.bfloat16),
            pltpu.VMEM((32, LANES * HEAD), jnp.bfloat16),
            pltpu.VMEM((32, PIX * PIX - LANES * HEAD + 2 * LANES), jnp.bfloat16),
            pltpu.VMEM((64, LANES), jnp.int32),
            pltpu.VMEM((8, LANES), f32),
        ),
        in_specs=[VMEM] * 4,
        out_specs=(VMEM,) * 5,
        name="prep",
    )(own, offsets, connections, confidence)
    head, tail = (lax.ppermute(v, "core", swap) for v in (head, tail))
    ready = pl.pallas_call(
        chip_kernel,
        out_shape=pltpu.VMEM((SUMS, 32, LANES), f32),
        in_specs=[VMEM] * 3,
        out_specs=VMEM,
        name="chip",
    )(kept(held), kept(head), kept(tail))
    pay = pl.pallas_call(
        match_kernel,
        out_shape=pltpu.VMEM((8, LANES), f32),
        in_specs=[VMEM] * 7,
        out_specs=VMEM,
        scratch_shapes=[pltpu.VMEM((SUMS, 64, LANES), f32)],
        name="match",
    )(*[kept(v) for v in (head, tail, prev, held, turn, ready, extra)])
    swaps = lambda first: [(i + d, i + 1 - d) for i in range(first, planes - 1, 2) for d in (0, 1)]
    odd_pairs = lax.ppermute(pay, "z", swaps(1))
    even_pairs = lax.ppermute(pay, "z", swaps(0))
    weights = pay[2:3] + odd_pairs[3:4] + even_pairs[4:5]
    block = jnp.concatenate([pay[0:2], odd_pairs[0:2], even_pairs[0:2], weights, jnp.zeros((1, LANES), f32)], 0)
    order = list(range(4 * PLANE))
    order[0], order[LEADER] = LEADER, 0
    gathered = lax.all_to_all(
        jnp.broadcast_to(block, (4 * PLANE, 8, LANES)),
        ("y", "core", "x"),
        0,
        0,
        tiled=True,
        axis_index_groups=[order],
    )
    sums, fields = pl.pallas_call(
        relax_kernel,
        out_shape=(
            pltpu.VMEM((planes, 1, LANES), f32),
            pltpu.VMEM((16, LANES), f32),
        ),
        in_specs=[VMEM],
        out_specs=(VMEM, VMEM),
        scratch_shapes=[
            pltpu.VMEM((14, LANES, LANES), jnp.bfloat16),
            pltpu.VMEM((WINDOW * 8, LANES), f32),
            pltpu.VMEM((WINDOW * 8, LANES), f32),
        ],
        name="relax",
    )(kept(gathered.reshape(32 * 8, LANES)))
    far = range(planes // 4, 3 * planes // 4)
    turned = [(i + planes // 2) % planes for i in range(planes)]
    mixed = [[2 * i + (1 - core if i in far else core) for i in turned] for core in (0, 1)]
    everywhere = lax.all_to_all(sums, ("z", "core"), 0, 0, tiled=True, axis_index_groups=mixed)
    measured, displacement = pl.pallas_call(
        finish_kernel,
        out_shape=(jax.ShapeDtypeStruct((2, 2, 1, 32), f32), jax.ShapeDtypeStruct((2, 1, 32), f32)),
        in_specs=[VMEM] * 2,
        out_specs=(VMEM, VMEM),
        name="finish",
    )(kept(everywhere), kept(fields))
    return (measured, displacement)


def solution(mesh):
    tiles = mesh.shape["tile"]
    devices = mesh.devices.reshape(mesh.shape["sec"] // PLANE, PLANE // 2, 2, tiles)
    return jax.shard_map(
        on_device,
        mesh=Mesh(devices, ("z", "y", "core", "x")),
        in_specs=(P(SEC, "x", None), P(None, None, SEC, "x"), P(None, SEC, "x"), P(SEC, "x")),
        out_specs=(P(None, None, SEC, "x"), P(None, SEC, "x")),
        check_vma=False,
    )
```

```python
import jax
import jax.numpy as jnp
from jax import lax
from jax.experimental import pallas as pl
from jax.experimental.pallas import tpu as pltpu
from jax.sharding import Mesh
from jax.sharding import PartitionSpec as P

PIX = 64
LANES = 128
TILES = PIX * PIX // LANES
REACH = 4
ROWS = 16
HEAD = 24
SUMS = 11
PLANE = 8
LEADER = 22
WINDOW = 3 * PLANE
ANCHOR = 0.05
SPRINGS = ((1, 1.0), (2, 0.5))
SEC = ("z", "y", "core")
VMEM = pl.BlockSpec(memory_space=pltpu.VMEM)


def kept(array):
    return pltpu.with_memory_space_constraint(array, pltpu.VMEM)


def lanes_of(rows):
    return lax.broadcasted_iota(jnp.int32, (rows, LANES), 1)


def sublanes_of(rows):
    return lax.broadcasted_iota(jnp.int32, (rows, LANES), 0)


def pick(values, index):
    return jnp.take_along_axis(values, index, axis=1, mode="promise_in_bounds")


def pick_rows(values, index):
    parts = [pick(values[8 * i : 8 * i + 8], index[8 * i : 8 * i + 8]) for i in range(values.shape[0] // 8)]
    return jnp.concatenate(parts, 0)


def shifted_tiles(tile_of, shift_rows, lane):
    steps = (shift_rows >> 1) + REACH
    odd_high = jnp.logical_and((shift_rows & 1) == 1, lane >= PIX)
    tiles = [tile_of((j + REACH) % TILES) for j in range(TILES)]
    for bit in range(4):
        move = (steps & (1 << bit)) != 0
        tiles = [jnp.where(move, tiles[(j - (1 << bit)) % TILES], tiles[j]) for j in range(TILES)]
    return [jnp.where(odd_high, tiles[j - 1], tiles[j]) for j in range(TILES)]


def rows_around(tile_of):
    low = lanes_of(ROWS) < PIX
    known = {}

    def rolled(j):
        j %= TILES
        if j not in known:
            known[j] = pltpu.roll(tile_of(j), PIX, 1)
        return known[j]

    return lambda j: (
        jnp.where(low, rolled(j - 1), rolled(j)),
        tile_of(j),
        jnp.where(low, rolled(j), rolled(j + 1)),
    )


def products(around, b_tile, shift_rows, shift_cols):
    lane = lanes_of(ROWS)
    moved = shifted_tiles(b_tile, shift_rows, lane)
    half = (lane ^ (PIX * (shift_rows & 1))) & PIX
    index = [half | ((lane - shift_cols - e) & (PIX - 1)) for e in (-1, 0, 1)]
    sums = [jnp.zeros((ROWS, LANES), jnp.float32)] * SUMS
    for j in range(TILES):
        rows_a = around(j)
        centre = rows_a[1]
        cols_b = [pick_rows(moved[j], index[e]) for e in range(3)]
        terms = [rows_a[e1] * cols_b[e2] for e1 in range(3) for e2 in range(3)]
        terms += [centre * centre, cols_b[1] * cols_b[1]]
        sums = [total + term for total, term in zip(sums, terms)]
    return sums


def tile_reader(refs, group):
    rows = slice(ROWS * group, ROWS * (group + 1))

    def tile(j):
        ref, j = (refs[0], j) if len(refs) == 1 or j < HEAD else (refs[1], j - HEAD)
        return ref[rows, LANES * j : LANES * (j + 1)].astype(jnp.float32)

    return tile


def pair_products(out, at, a_refs, b_refs, turn, faces=None):
    for g in range(2):
        rows = slice(ROWS * g, ROWS * (g + 1))
        if faces is None:
            around = rows_around(tile_reader(a_refs, g))
        else:
            around = lambda j, rows=rows: [faces[e, rows, LANES * j : LANES * (j + 1)] for e in range(3)]
        sums = products(around, tile_reader(b_refs, g), turn(0, rows), turn(1, rows))
        for k in range(SUMS):
            out[k, at + ROWS * g : at + ROWS * (g + 1), :] = sums[k]


def own_turns(turn):
    return lambda part, rows: turn[32 * part + rows.start : 32 * part + rows.stop, :]


def sent_turns(tail):
    at = PIX * PIX - LANES * HEAD
    return lambda part, rows: (
        tail[rows, at + LANES * part : at + LANES * (part + 1)].astype(jnp.float32).astype(jnp.int32)
    )


def prep_kernel(pixels, offsets, connections, confidence, own, head, tail, turn, extra):
    cut = LANES * HEAD
    rest = PIX * PIX - cut
    own[...] = pixels[...]
    head[...] = pixels[:, 0:cut]
    tail[:, 0:rest] = pixels[:, cut:]
    patch = lax.broadcasted_iota(jnp.int32, (32, 32), 0)
    diagonal = patch == lax.broadcasted_iota(jnp.int32, (32, 32), 1)
    for d in range(2):
        for part in range(2):
            chosen = jnp.where(diagonal, offsets[d, part].astype(jnp.float32), 0.0)
            column = jnp.broadcast_to(jnp.sum(chosen, axis=1, keepdims=True), (32, LANES))
            if d == 0:
                tail[:, rest + LANES * part : rest + LANES * (part + 1)] = column.astype(jnp.bfloat16)
            else:
                turn[32 * part : 32 * (part + 1), :] = column.astype(jnp.int32)
    extra[...] = jnp.zeros_like(extra)
    for j in range(4):
        extra[1:2, 32 * j : 32 * (j + 1)] = connections[j].astype(jnp.float32)
    for k in range(3):
        extra[2 + k : 3 + k, 32 * k : 32 * (k + 1)] = confidence[...]


def chip_kernel(own, head, tail, ready, faces):
    for g in range(2):
        around = rows_around(tile_reader((own,), g))
        for j in range(TILES):
            for e, face in enumerate(around(j)):
                faces[e, ROWS * g : ROWS * (g + 1), LANES * j : LANES * (j + 1)] = face

    @pl.when(lax.axis_index("core") == 0)
    def _():
        pair_products(ready, 0, (head, tail), (own,), sent_turns(tail))


def match_kernel(head, tail, prev, faces, turn, ready, extra, pay, sums):
    core = lax.axis_index("core")

    @pl.when(core == 0)
    def _():
        sums[:, 32:64, :] = ready[...]

    @pl.when(core != 0)
    def _():
        pair_products(sums, 32, (head, tail), (prev,), sent_turns(tail))

    pair_products(sums, 0, None, (prev,), own_turns(turn), faces)
    total = [jnp.sum(sums[k], axis=1, keepdims=True) for k in range(SUMS)]
    scale = (total[9] / PIX**2 + 1e-05) * (total[10] / PIX**2 + 1e-05) * PIX**2
    inverse = 1.0 / scale
    weights = [[total[3 * e1 + e2] * total[3 * e1 + e2] * inverse for e2 in range(3)] for e1 in range(3)]
    row_sums = [weights[e][0] + weights[e][1] + weights[e][2] for e in range(3)]
    share = 1.0 / (1.0 + row_sums[0] + row_sums[1] + row_sums[2])
    col_low = weights[0][0] + weights[1][0] + weights[2][0]
    col_high = weights[0][2] + weights[1][2] + weights[2][2]
    shifts = [
        jnp.concatenate([turns(part, slice(0, 32)) for turns in (own_turns(turn), sent_turns(tail))], 0).astype(jnp.float32)
        for part in range(2)
    ]
    found_rows = shifts[0] + (row_sums[2] - row_sums[0]) * share
    found_cols = shifts[1] + (col_high - col_low) * share
    lane, pair = lanes_of(64), sublanes_of(64)
    line = jnp.where(lane == pair, found_rows, jnp.where(lane == 64 + pair, found_cols, 0.0))
    pay[...] = extra[...]
    pay[0:1, :] = jnp.sum(line, axis=0, keepdims=True)


def relax_kernel(gathered, sums_out, fields_out, links, left, pushed):
    lane = lanes_of(PLANE)
    sub = sublanes_of(PLANE)

    z, y, core, x_own = (lax.axis_index(name) for name in ("z", "y", "core", "x"))
    even = z % 2 == 0

    def loaded(row):
        found = [gathered[pl.ds(8 * x + row, PLANE, stride=32), :] for x in range(4)]
        section, x = LEADER // 4, LEADER % 4
        first, other = found[0], found[x]
        found[0] = jnp.where(sub == 0, pltpu.roll(other, PLANE - section, 0), first)
        found[x] = jnp.where(sub == section, pltpu.roll(first, section, 0), other)
        return found

    def assembled(parts, quarter):
        total = jnp.zeros((PLANE, LANES), jnp.float32)
        for x in range(4):
            moved = pltpu.roll(parts[x], 32 * ((x - quarter) % 4), 1) if x != quarter else parts[x]
            total = jnp.where(lane // 32 == x, moved, total)
        return total

    def in_order(own, odd_pair, even_pair):
        return (jnp.where(even, odd_pair, even_pair), own, jnp.where(even, even_pair, odd_pair))

    def windows(row):
        parts = [in_order(*[loaded(row + 2 * k)[x] for k in range(3)]) for x in range(4)]
        join = lambda q: jnp.concatenate([assembled([parts[x][p] for x in range(4)], q) for p in range(3)], 0)
        return [join(q) for q in range(4)]

    def cores_swapped(values):
        even = sublanes_of(WINDOW) % 2 == 0
        return jnp.where(even, up(values, 1), down(values, 1))

    up = lambda v, k: pltpu.roll(v, v.shape[0] - k, 0)
    down = lambda v, k: pltpu.roll(v, k, 0)

    found = windows(0)
    measured = {1: [cores_swapped(found[1]), cores_swapped(found[3])], 2: [found[0], found[2]]}
    node_links = [links_of.astype(jnp.int32) for links_of in windows(1)]
    weights = loaded(6)
    confidence = jnp.concatenate(in_order(*[assembled(weights, q) for q in range(3)]), 0)
    section = PLANE * (z - 1) + sublanes_of(WINDOW)
    chain = {d: jnp.where(section >= d, confidence, 0.0) for d, _ in SPRINGS}

    first, last = 4, 18
    node = lax.broadcasted_iota(jnp.int32, (LANES, LANES), 0)
    for s in range(first, last):
        ends = [jnp.where(node == node_links[j][s : s + 1], 1.0, 0.0) for j in range(4)]
        links[s - first] = ((ends[0] + ends[1]) + (ends[2] + ends[3])).astype(jnp.bfloat16)

    def pushed_along(field, begin, end):
        for c in range(2):
            rest = field[c]
            for part in range(3):
                rounded = rest.astype(jnp.bfloat16).astype(jnp.float32)
                left[pl.ds(2 * part + c, WINDOW, stride=8), :] = rounded
                rest = rest - rounded
        for s in range(begin, end):
            pushed[8 * s : 8 * s + 8, :] = lax.dot_general(
                left[8 * s : 8 * s + 8, :].astype(jnp.bfloat16),
                links[s - first],
                (((1,), (1,)), ((), ())),
                preferred_element_type=jnp.float32,
            )
        part = lambda k: pushed[pl.ds(k, WINDOW, stride=8), :]
        return [part(c) + part(2 + c) + part(4 + c) for c in range(2)]

    def image(field, begin, end, degree):
        back = pushed_along(field, begin, end)
        if degree is None:
            degree = pushed[pl.ds(6, WINDOW, stride=8), :]
        out = []
        for c in range(2):
            v = field[c]
            ahead = [pick_rows(v, node_links[j]) for j in range(4)]
            plane = (4.0 + degree) * v - ((ahead[0] + ahead[1]) + (ahead[2] + ahead[3])) - back[c]
            total = plane + ANCHOR * v
            for d, spring in SPRINGS:
                term = chain[d] * (v - down(v, d))
                total = total + spring * (term - up(term, d))
            out.append(total)
        return out, degree

    left[...] = jnp.ones_like(left)
    pushed[...] = jnp.zeros_like(pushed)
    start = []
    for c in range(2):
        total = jnp.zeros((WINDOW, LANES), jnp.float32)
        for d, spring in SPRINGS:
            term = chain[d] * measured[d][c]
            total = total + spring * (up(term, d) - term)
        start.append(total)
    once, degree = image(start, 4, 18, None)
    twice, _ = image(once, 6, 16, degree)

    mid = lambda v: v[PLANE : 2 * PLANE]
    dot = lambda a, b: mid(a[0]) * mid(b[0]) + mid(a[1]) * mid(b[1])
    sums = [dot(start, start), dot(start, once), dot(once, once), dot(once, twice), dot(twice, twice)]
    form = ANCHOR * sums[4]
    for c in range(2):
        v = twice[c]
        for j in range(4):
            differ = mid(v) - pick(mid(v), mid(node_links[j]))
            form = form + differ * differ
        for d, spring in SPRINGS:
            differ = mid(v - down(v, d))
            form = form + spring * mid(chain[d]) * differ * differ
    sums.append(form)
    rows = [jnp.sum(s, axis=0, keepdims=True) for s in sums]
    rows = jnp.concatenate(rows + [jnp.zeros((2, LANES), jnp.float32)], 0)
    totals = jnp.sum(rows, axis=1, keepdims=True)
    line = jnp.sum(jnp.where(lane == sub, totals, 0.0), axis=0, keepdims=True)
    sums_out[...] = jnp.broadcast_to(line[None], sums_out.shape)

    mine = sub == 2 * y + core

    def own(v):
        row = jnp.sum(jnp.where(mine, mid(v), 0.0), axis=0, keepdims=True)
        return pltpu.roll(row, (LANES - 32 * x_own) % LANES, 1)

    fields = [own(f[c]) for f in (start, once, twice) for c in range(2)]
    fields += [own(measured[d][c]) for d in (1, 2) for c in range(2)]
    fields_out[...] = jnp.concatenate(fields + [jnp.zeros((6, LANES), jnp.float32)], 0)


def finish_kernel(sums, fields, measured_out, out):
    for d in range(2):
        for c in range(2):
            row = 6 + 2 * d + c
            measured_out[d, c] = fields[row : row + 1, 0:32]
    line = jnp.sum(sums[...], axis=0)
    lane = lanes_of(1)
    m = [jnp.sum(jnp.where(lane == k, line, 0.0), axis=1, keepdims=True) for k in range(6)]
    bounded = lambda top, below: jnp.clip(top / below, 0.0, 1.0 / ANCHOR)
    a0 = m[0] / m[1]
    norm = m[0] - 2.0 * a0 * m[1] + a0 * a0 * m[2]
    curve = m[1] - 2.0 * a0 * m[2] + a0 * a0 * m[3]
    a1 = bounded(norm, curve)
    p, q = a0 + a1, a0 * a1
    k1, k2, k3, k4 = -2.0 * p, p * p + 2.0 * q, -2.0 * p * q, q * q
    norm = m[0] + k1 * m[1] + k2 * m[2] + k3 * m[3] + k4 * m[4]
    curve = m[1] + k1 * m[2] + k2 * m[3] + k3 * m[4] + k4 * m[5]
    a2 = bounded(norm, curve)
    for c in range(2):
        v0, v1, v2 = (fields[2 * k + c : 2 * k + c + 1, :] for k in range(3))
        value = (q + a2 * p) * v1 - (p + a2) * v0 - (a2 * q) * v2
        out[c] = value[:, :32]


def on_device(pixels, offsets, connections, confidence):
    planes = lax.axis_size("z")
    count = planes * PLANE
    own = pixels[0]
    swap = [(0, 1), (1, 0)]
    prev = lax.ppermute(own, SEC, [(i, i + 2) for i in range(count - 2)])
    f32 = jnp.float32
    held, head, tail, turn, extra = pl.pallas_call(
        prep_kernel,
        out_shape=(
            pltpu.VMEM((32, PIX * PIX), jnp.bfloat16),
            pltpu.VMEM((32, LANES * HEAD), jnp.bfloat16),
            pltpu.VMEM((32, PIX * PIX - LANES * HEAD + 2 * LANES), jnp.bfloat16),
            pltpu.VMEM((64, LANES), jnp.int32),
            pltpu.VMEM((8, LANES), f32),
        ),
        in_specs=[VMEM] * 4,
        out_specs=(VMEM,) * 5,
        name="prep",
    )(own, offsets, connections, confidence)
    head, tail = (lax.ppermute(v, "core", swap) for v in (head, tail))
    ready, faces = pl.pallas_call(
        chip_kernel,
        out_shape=(pltpu.VMEM((SUMS, 32, LANES), f32), pltpu.VMEM((3, 32, PIX * PIX), f32)),
        in_specs=[VMEM] * 3,
        out_specs=(VMEM, VMEM),
        name="chip",
    )(kept(held), kept(head), kept(tail))
    pay = pl.pallas_call(
        match_kernel,
        out_shape=pltpu.VMEM((8, LANES), f32),
        in_specs=[VMEM] * 7,
        out_specs=VMEM,
        scratch_shapes=[pltpu.VMEM((SUMS, 64, LANES), f32)],
        name="match",
    )(*[kept(v) for v in (head, tail, prev, faces, turn, ready, extra)])
    swaps = lambda first: [(i + d, i + 1 - d) for i in range(first, planes - 1, 2) for d in (0, 1)]
    odd_pairs = lax.ppermute(pay, "z", swaps(1))
    even_pairs = lax.ppermute(pay, "z", swaps(0))
    weights = pay[2:3] + odd_pairs[3:4] + even_pairs[4:5]
    block = jnp.concatenate([pay[0:2], odd_pairs[0:2], even_pairs[0:2], weights, jnp.zeros((1, LANES), f32)], 0)
    order = list(range(4 * PLANE))
    order[0], order[LEADER] = LEADER, 0
    gathered = lax.all_to_all(
        jnp.broadcast_to(block, (4 * PLANE, 8, LANES)),
        ("y", "core", "x"),
        0,
        0,
        tiled=True,
        axis_index_groups=[order],
    )
    sums, fields = pl.pallas_call(
        relax_kernel,
        out_shape=(
            pltpu.VMEM((planes, 1, LANES), f32),
            pltpu.VMEM((16, LANES), f32),
        ),
        in_specs=[VMEM],
        out_specs=(VMEM, VMEM),
        scratch_shapes=[
            pltpu.VMEM((14, LANES, LANES), jnp.bfloat16),
            pltpu.VMEM((WINDOW * 8, LANES), f32),
            pltpu.VMEM((WINDOW * 8, LANES), f32),
        ],
        name="relax",
    )(kept(gathered.reshape(32 * 8, LANES)))
    turned = [[(i + planes // 2) % planes for i in range(planes)]]
    everywhere = lax.all_to_all(sums, "z", 0, 0, tiled=True, axis_index_groups=turned)
    measured, displacement = pl.pallas_call(
        finish_kernel,
        out_shape=(jax.ShapeDtypeStruct((2, 2, 1, 32), f32), jax.ShapeDtypeStruct((2, 1, 32), f32)),
        in_specs=[VMEM] * 2,
        out_specs=(VMEM, VMEM),
        name="finish",
    )(kept(everywhere), kept(fields))
    return (measured, displacement)


def solution(mesh):
    tiles = mesh.shape["tile"]
    devices = mesh.devices.reshape(mesh.shape["sec"] // PLANE, PLANE // 2, 2, tiles)
    return jax.shard_map(
        on_device,
        mesh=Mesh(devices, ("z", "y", "core", "x")),
        in_specs=(P(SEC, "x", None), P(None, None, SEC, "x"), P(None, SEC, "x"), P(SEC, "x")),
        out_specs=(P(None, None, SEC, "x"), P(None, SEC, "x")),
        check_vma=False,
    )
```
